512 devices in a mesh: lat: 16 (over z_lo, y), lon: 32 (over x, z_hi, core).
Axes of the slice: x: 4, y: 8, z: 8 (z_hi: 4, z_lo: 2; z = z_hi * 2 + z_lo), core: 2. Of those that a mesh axis runs over, the one named last changes fastest.
Arguments:
- fine_tokens: bfloat16 [288, 768, 512], P('lat', 'lon'), may hold values from -6 to 6
- cotangent: bfloat16 [288, 768, 512], P('lat', 'lon'), may hold values from -6 to 6
- norm_gain: float32 [512], replicated, may hold values from 0.1 to 1.9
- qkv_weight: bfloat16 [512, 1536], replicated
- qkv_down: bfloat16 [512, 8], replicated, may hold values from -0.25 to 0.25
- qkv_up: bfloat16 [8, 1536], replicated, may hold values from -2 to 2
- out_weight: bfloat16 [512, 512], replicated, may hold values from -0.25 to 0.25
- out_down: bfloat16 [512, 8], replicated, may hold values from -0.25 to 0.25
- out_up: bfloat16 [8, 512], replicated, may hold values from -2 to 2
Outputs:
- mixed: bfloat16 [288, 768, 512], P('lat', 'lon')
- grad_in: bfloat16 [288, 768, 512], P('lat', 'lon')
- grad_qkv_down: float32 [512, 8], replicated
- grad_qkv_up: float32 [8, 1536], replicated
- grad_out_down: float32 [512, 8], replicated
- grad_out_up: float32 [8, 512], replicated
The draws below stay inside these ranges and needn't reach their ends.
All inputs are finite; a program needn't handle non-finite values.
Results may differ from the reference program's by a relative error of at most 0.017.
The reference program's roundings to bfloat16 on the way count: a program that leaves them out, or rounds other values in their place, can miss the bound.
Values may be sent and summed in bfloat16 or wider, within the bound.
No kernel may reach another device: no remote copies, remote signals or barrier semaphores. Data moves between devices by JAX's collectives and lax.ppermute only.
A program may use at most 64 MiB of HBM per device.

```python
import math
import jax
import jax.numpy as jnp
from jax import lax

D = 512
HEADS = 16
RANK = 8
WIN_LAT = 6
WIN_LON = 12
NLAT = 288
NLON = 768


def draw_qkv_weight(key, part):
    key = jax.random.fold_in(key, 17)
    base = jax.random.normal(key, (D, 3 * D), jnp.float32) / math.sqrt(D)
    return base.astype(jnp.bfloat16)


def steps_of(stream_key, dims, shards, smallest, largest):
    level, own = 1.0, jax.random.fold_in(stream_key, 6)
    for axis_at, blocks in shards:
        steps = jnp.exp(jax.random.uniform(jax.random.fold_in(own, axis_at), (blocks,), jnp.float32, smallest / len(shards), largest / len(shards)))
        level = level * jnp.repeat(steps, dims[axis_at] // blocks).reshape([-1 if axis == axis_at else 1 for axis in range(len(dims))])
    return level


def scatter_about(stream_key, extent, scale, most, cuts=(), kind=jnp.bfloat16):
    factor_of = steps_of(stream_key, extent, cuts, -0.22, 0.18) if cuts else 1.0
    result = jax.random.normal(stream_key, extent, jnp.float32) * scale * factor_of
    return jnp.minimum(jnp.maximum(result, -most), most).astype(kind)


def setup_inputs(seed: int = 0) -> dict:
    seeds = jax.random.split(jax.random.key(seed), 10)
    return {
        "fine_tokens": scatter_about(seeds[0], (NLAT, NLON, D), 1.0, 6.0, ((0, 16), (1, 32))),
        "cotangent": scatter_about(seeds[1], (NLAT, NLON, D), 1.0, 6.0, ((0, 16), (1, 32))),
        "norm_gain": jnp.clip(1.0 + 0.18 * jax.random.normal(seeds[2], (D,), jnp.float32), 0.1, 1.9),
        "qkv_weight": draw_qkv_weight(jax.random.fold_in(seeds[9], 71), 0),
        "qkv_down": scatter_about(seeds[4], (D, RANK), D ** -0.5, 0.25),
        "qkv_up": scatter_about(seeds[5], (RANK, 3 * D), RANK ** -0.5, 2.0),
        "out_weight": scatter_about(seeds[6], (D, D), D ** -0.5, 0.25),
        "out_down": scatter_about(seeds[7], (D, RANK), D ** -0.5, 0.25),
        "out_up": scatter_about(seeds[8], (RANK, D), RANK ** -0.5, 2.0),
    }


def layer_norm(widened, norm_gain):
    center = widened - lax.optimization_barrier(jnp.mean(widened, axis=-1, keepdims=True))
    spread = lax.optimization_barrier(jnp.mean(center * center, axis=-1, keepdims=True))
    return center * lax.rsqrt(spread + 1e-05) * norm_gain.astype(jnp.float32)

def inner_product(left, right):
    return lax.dot_general(left, right, (((0,), (0,)), ((), ())), preferred_element_type=jnp.float32)

def times_transpose(left, right):
    return lax.dot_general(left, right, (((1,), (1,)), ((), ())), preferred_element_type=jnp.float32)

def window_attention(packed, pole_side):
    lat_cells, lon_cells, triple = packed.shape
    features = triple // 3
    head_width = features // HEADS
    lat_windows = lat_cells // WIN_LAT
    lon_windows = lon_cells // WIN_LON
    window_cells = WIN_LAT * WIN_LON
    window_tiles = packed.reshape(lat_windows, WIN_LAT, lon_windows, WIN_LON, 3, HEADS, head_width)
    window_tiles = window_tiles.transpose(0, 2, 4, 5, 1, 3, 6).reshape(lat_windows, lon_windows, 3, HEADS, window_cells, head_width)
    queries = window_tiles[:, :, 0]
    key_rows = window_tiles[:, :, 1]
    value_rows = window_tiles[:, :, 2]
    scores = jnp.einsum('abhqd,abhkd->abhqk', queries, key_rows, preferred_element_type=jnp.float32) / math.sqrt(head_width)
    pole_rows = jnp.broadcast_to(pole_side.reshape(lat_windows, WIN_LAT, 1), (lat_windows, WIN_LAT, WIN_LON)).reshape(lat_windows, 1, window_cells)
    allowed = pole_rows[:, :, :, None] == pole_rows[:, :, None, :]
    scores = jnp.where(allowed[:, :, None], scores, -1e+30)
    row_top = lax.optimization_barrier(jnp.max(scores, axis=-1, keepdims=True))
    exponent = jnp.exp(scores - row_top)
    weights = (exponent / lax.optimization_barrier(jnp.sum(exponent, axis=-1, keepdims=True))).astype(jnp.bfloat16)
    blended = jnp.einsum('abhqk,abhkd->abhqd', weights, value_rows, preferred_element_type=jnp.float32).astype(jnp.bfloat16)
    blended = blended.reshape(lat_windows, lon_windows, HEADS, WIN_LAT, WIN_LON, head_width).transpose(0, 3, 1, 4, 2, 5)
    return blended.reshape(lat_cells * lon_cells, features)

def forward(shifted, pole_side, norm_gain, weight_set):
    qkv_weight, qkv_down, qkv_up, out_weight, out_down, out_up = weight_set
    lat_cells, lon_cells, features = shifted.shape
    widened = shifted.astype(jnp.float32).reshape(lat_cells * lon_cells, features)
    normed, norm_back = jax.vjp(lambda argument: layer_norm(argument, norm_gain), widened)
    hidden_in = normed.astype(jnp.bfloat16)
    low_query = jnp.dot(hidden_in, qkv_down, preferred_element_type=jnp.float32).astype(jnp.bfloat16)
    packed = (jnp.dot(hidden_in, qkv_weight, preferred_element_type=jnp.float32) + jnp.dot(low_query, qkv_up, preferred_element_type=jnp.float32)).astype(jnp.bfloat16)
    blended, attend_back = jax.vjp(lambda argument: window_attention(argument.reshape(lat_cells, lon_cells, 3 * features), pole_side), packed)
    low_out = jnp.dot(blended, out_down, preferred_element_type=jnp.float32).astype(jnp.bfloat16)
    update = (jnp.dot(blended, out_weight, preferred_element_type=jnp.float32) + jnp.dot(low_out, out_up, preferred_element_type=jnp.float32)).astype(jnp.bfloat16)
    return (update.reshape(lat_cells, lon_cells, features), (hidden_in, low_query, blended, low_out, norm_back, attend_back))

def backward(saved, shifted_cot, weight_set):
    qkv_weight, qkv_down, qkv_up, out_weight, out_down, out_up = weight_set
    hidden_in, low_query, blended, low_out, norm_back, attend_back = saved
    lat_cells, lon_cells, features = shifted_cot.shape
    upstream = shifted_cot.reshape(lat_cells * lon_cells, features)
    grad_up_out = inner_product(low_out, upstream)
    back_low_out = times_transpose(upstream, out_up).astype(jnp.bfloat16)
    grad_down_out = inner_product(blended, back_low_out)
    back_blended = (times_transpose(upstream, out_weight) + times_transpose(back_low_out, out_down)).astype(jnp.bfloat16)
    back_packed = attend_back(back_blended)[0]
    grad_up_qkv = inner_product(low_query, back_packed)
    back_low_query = times_transpose(back_packed, qkv_up).astype(jnp.bfloat16)
    grad_down_qkv = inner_product(hidden_in, back_low_query)
    back_hidden = times_transpose(back_packed, qkv_weight) + times_transpose(back_low_query, qkv_down)
    back_tokens = norm_back(back_hidden)[0].astype(jnp.bfloat16)
    return (back_tokens.reshape(lat_cells, lon_cells, features), (grad_down_qkv, grad_up_qkv, grad_down_out, grad_up_out))

def reference(fine_tokens, cotangent, norm_gain, qkv_weight, qkv_down, qkv_up, out_weight, out_down, out_up):
    weight_set = (qkv_weight, qkv_down, qkv_up, out_weight, out_down, out_up)
    half_lat = WIN_LAT // 2
    half_lon = WIN_LON // 2
    shifted = jnp.roll(fine_tokens, (-half_lat, -half_lon), axis=(0, 1))
    shifted_cot = jnp.roll(cotangent, (-half_lat, -half_lon), axis=(0, 1))
    pole_side = (jnp.arange(NLAT, dtype=jnp.int32) + half_lat >= NLAT).astype(jnp.int32)
    bands = NLAT // WIN_LAT

    def one_band(band_item):
        band_tokens, band_cot, band_side = band_item
        update, saved = forward(band_tokens, band_side, norm_gain, weight_set)
        back_tokens, grads = backward(saved, band_cot, weight_set)
        mixed_band = (band_tokens.astype(jnp.float32) + update.astype(jnp.float32)).astype(jnp.bfloat16)
        grad_band = (band_cot.astype(jnp.float32) + back_tokens.astype(jnp.float32)).astype(jnp.bfloat16)
        return (mixed_band, grad_band, grads)
    mixed_s, grad_s, grads = lax.map(one_band, (shifted.reshape(bands, WIN_LAT, NLON, D), shifted_cot.reshape(bands, WIN_LAT, NLON, D), pole_side.reshape(bands, WIN_LAT)))
    mixed = jnp.roll(mixed_s.reshape(NLAT, NLON, D), (half_lat, half_lon), axis=(0, 1))
    grad_in = jnp.roll(grad_s.reshape(NLAT, NLON, D), (half_lat, half_lon), axis=(0, 1))
    scale = 1.0 / math.sqrt(NLAT * NLON)
    grad_qkv_down = lax.optimization_barrier(jnp.sum(grads[0], axis=0)) * scale
    grad_qkv_up = lax.optimization_barrier(jnp.sum(grads[1], axis=0)) * scale
    grad_out_down = lax.optimization_barrier(jnp.sum(grads[2], axis=0)) * scale
    grad_out_up = lax.optimization_barrier(jnp.sum(grads[3], axis=0)) * scale
    return (mixed, grad_in, grad_qkv_down, grad_qkv_up, grad_out_down, grad_out_up)
```

```python
import math

import jax
import jax.numpy as jnp
from jax import lax
from jax.sharding import PartitionSpec as P

HEADS = 16
WIN_LAT = 6
WIN_LON = 12


def shifted_2(block, axis, distance):
    devices = range(lax.axis_size(axis))
    route = [((i - distance) % len(devices), i) for i in devices]
    return lax.ppermute(block, axis, route)


def layer_norm(widened, norm_gain):
    center = widened - jnp.mean(widened, axis=-1, keepdims=True)
    spread = jnp.mean(center * center, axis=-1, keepdims=True)
    return center * lax.rsqrt(spread + 1e-05) * norm_gain


def inner_product(left, right):
    return lax.dot_general(
        left, right, (((0,), (0,)), ((), ())), preferred_element_type=jnp.float32
    )


def times_transpose(left, right):
    return lax.dot_general(
        left, right, (((1,), (1,)), ((), ())), preferred_element_type=jnp.float32
    )


def window_attention(packed, pole_side):
    lat_cells, lon_cells, triple = packed.shape
    features = triple // 3
    head_width = features // HEADS
    lat_windows = lat_cells // WIN_LAT
    lon_windows = lon_cells // WIN_LON
    window_cells = WIN_LAT * WIN_LON
    window_tiles = packed.reshape(lat_windows, WIN_LAT, lon_windows, WIN_LON, 3, HEADS, head_width)
    window_tiles = window_tiles.transpose(0, 2, 4, 5, 1, 3, 6).reshape(
        lat_windows, lon_windows, 3, HEADS, window_cells, head_width
    )
    queries = window_tiles[:, :, 0]
    key_rows = window_tiles[:, :, 1]
    value_rows = window_tiles[:, :, 2]
    scores = jnp.einsum(
        "abhqd,abhkd->abhqk", queries, key_rows, preferred_element_type=jnp.float32
    ) / math.sqrt(head_width)
    pole_rows = jnp.broadcast_to(
        pole_side.reshape(lat_windows, WIN_LAT, 1), (lat_windows, WIN_LAT, WIN_LON)
    ).reshape(lat_windows, 1, window_cells)
    allowed = pole_rows[:, :, :, None] == pole_rows[:, :, None, :]
    scores = jnp.where(allowed[:, :, None], scores, -1e30)
    row_top = jnp.max(scores, axis=-1, keepdims=True)
    exponent = jnp.exp(scores - row_top)
    weights = (exponent / jnp.sum(exponent, axis=-1, keepdims=True)).astype(jnp.bfloat16)
    blended = jnp.einsum(
        "abhqk,abhkd->abhqd", weights, value_rows, preferred_element_type=jnp.float32
    ).astype(jnp.bfloat16)
    blended = blended.reshape(
        lat_windows, lon_windows, HEADS, WIN_LAT, WIN_LON, head_width
    ).transpose(0, 3, 1, 4, 2, 5)
    return blended.reshape(lat_cells * lon_cells, features)


def forward(shifted, pole_side, norm_gain, weight_set):
    qkv_weight, qkv_down, qkv_up, out_weight, out_down, out_up = weight_set
    lat_cells, lon_cells, features = shifted.shape
    widened = shifted.astype(jnp.float32).reshape(lat_cells * lon_cells, features)
    normed, norm_back = jax.vjp(lambda argument: layer_norm(argument, norm_gain), widened)
    hidden_in = normed.astype(jnp.bfloat16)
    low_query = jnp.dot(hidden_in, qkv_down, preferred_element_type=jnp.float32).astype(
        jnp.bfloat16
    )
    packed = (
        jnp.dot(hidden_in, qkv_weight, preferred_element_type=jnp.float32)
        + jnp.dot(low_query, qkv_up, preferred_element_type=jnp.float32)
    ).astype(jnp.bfloat16)
    blended, attend_back = jax.vjp(
        lambda argument: window_attention(
            argument.reshape(lat_cells, lon_cells, 3 * features), pole_side
        ),
        packed,
    )
    low_out = jnp.dot(blended, out_down, preferred_element_type=jnp.float32).astype(jnp.bfloat16)
    update = (
        jnp.dot(blended, out_weight, preferred_element_type=jnp.float32)
        + jnp.dot(low_out, out_up, preferred_element_type=jnp.float32)
    ).astype(jnp.bfloat16)
    return (
        update.reshape(lat_cells, lon_cells, features),
        (hidden_in, low_query, blended, low_out, norm_back, attend_back),
    )


def backward(saved, shifted_cot, weight_set):
    qkv_weight, qkv_down, qkv_up, out_weight, out_down, out_up = weight_set
    hidden_in, low_query, blended, low_out, norm_back, attend_back = saved
    lat_cells, lon_cells, features = shifted_cot.shape
    upstream = shifted_cot.reshape(lat_cells * lon_cells, features)
    grad_up_out = inner_product(low_out, upstream)
    back_low_out = times_transpose(upstream, out_up).astype(jnp.bfloat16)
    grad_down_out = inner_product(blended, back_low_out)
    back_blended = (
        times_transpose(upstream, out_weight) + times_transpose(back_low_out, out_down)
    ).astype(jnp.bfloat16)
    back_packed = attend_back(back_blended)[0]
    grad_up_qkv = inner_product(low_query, back_packed)
    back_low_query = times_transpose(back_packed, qkv_up).astype(jnp.bfloat16)
    grad_down_qkv = inner_product(hidden_in, back_low_query)
    back_hidden = times_transpose(back_packed, qkv_weight) + times_transpose(
        back_low_query, qkv_down
    )
    back_tokens = norm_back(back_hidden)[0].astype(jnp.bfloat16)
    return (
        back_tokens.reshape(lat_cells, lon_cells, features),
        (grad_down_qkv, grad_up_qkv, grad_down_out, grad_up_out),
    )


def roll_rows(field, step_dir):
    half = WIN_LAT // 2
    piece = field[..., :half, :, :] if step_dir < 0 else field[..., -half:, :, :]
    kept = field[..., half:, :, :] if step_dir < 0 else field[..., :-half, :, :]
    moved = shifted_2(piece, "lat", step_dir)
    return jnp.concatenate((kept, moved) if step_dir < 0 else (moved, kept), axis=-3)


def roll_columns(field, step_dir):
    half = WIN_LON // 2
    piece = field[..., :half, :] if step_dir < 0 else field[..., -half:, :]
    kept = field[..., half:, :] if step_dir < 0 else field[..., :-half, :]
    moved = shifted_2(piece, "lon", step_dir)
    return jnp.concatenate((kept, moved) if step_dir < 0 else (moved, kept), axis=-2)


def into_windows(field):
    return roll_rows(roll_columns(field, -1), -1)


def out_of_windows(field):
    return roll_columns(roll_rows(field, 1), 1)


def add_round(first, second):
    return (first.astype(jnp.float32) + second.astype(jnp.float32)).astype(jnp.bfloat16)


def exchange(tiles, axis):
    return lax.all_to_all(tiles, axis, 0, 0, tiled=True)


def gather_tiles(tile, axis):
    spread = jnp.broadcast_to(tile[None], (lax.axis_size(axis),) + tile.shape)
    return exchange(spread, axis)


def total_over_mesh(packed):
    rows, width = packed.shape
    owners = lax.axis_size("lon")
    tiles = jnp.pad(packed, ((0, 0), (0, owners * 128 - width)))
    tiles = tiles.reshape(rows, owners, 128).transpose(1, 0, 2)
    own = jnp.sum(exchange(tiles, "lon"), axis=0)
    own = jnp.sum(gather_tiles(own, "lat"), axis=0)
    tiles = gather_tiles(own, "lon")
    return tiles.transpose(1, 0, 2).reshape(rows, owners * 128)[:, :width]


def shards(
    fine_tokens, cotangent, norm_gain, qkv_weight, qkv_down, qkv_up, out_weight, out_down, out_up
):
    weight_set = (qkv_weight, qkv_down, qkv_up, out_weight, out_down, out_up)
    lat_cells, lon_cells, features = fine_tokens.shape
    total_rows = lat_cells * lax.axis_size("lat")
    first_row = lax.axis_index("lat") * lat_cells
    pole_side = (
        first_row + jnp.arange(lat_cells, dtype=jnp.int32) + WIN_LAT // 2 >= total_rows
    ).astype(jnp.int32)
    shifted = into_windows(fine_tokens)
    update, saved = forward(shifted, pole_side, norm_gain, weight_set)
    mixed = add_round(fine_tokens, out_of_windows(update))
    shifted_cot = into_windows(cotangent)
    back_tokens, grads = backward(saved, shifted_cot, weight_set)
    grad_in = add_round(cotangent, out_of_windows(back_tokens))
    scale = 1.0 / math.sqrt(total_rows * lon_cells * lax.axis_size("lon"))
    out_packed = lax.psum(jnp.concatenate((grads[2].T, grads[3]), axis=1), ("lat", "lon"))
    qkv_packed = total_over_mesh(jnp.concatenate((grads[0].T, grads[1]), axis=1)) * scale
    out_packed = out_packed * scale
    return (
        mixed,
        grad_in,
        qkv_packed[:, :features].T,
        qkv_packed[:, features:],
        out_packed[:, :features].T,
        out_packed[:, features:],
    )


def solution(mesh):
    in_specs = (P("lat", "lon", None), P("lat", "lon", None), P(), P(), P(), P(), P(), P(), P())
    out_specs = (P("lat", "lon", None), P("lat", "lon", None), P(), P(), P(), P())
    return jax.shard_map(shards, mesh=mesh, in_specs=in_specs, out_specs=out_specs, check_vma=False)
```

```python
import math

import jax
import jax.numpy as jnp
from jax import lax
from jax.experimental import pallas as pl
from jax.experimental.pallas import tpu as pltpu
from jax.sharding import PartitionSpec as P

HEADS = 16
WIN_LAT = 6
WIN_LON = 12
HALF_LAT = WIN_LAT // 2
HALF_LON = WIN_LON // 2
LAT_CELLS = 18
LON_CELLS = 24
D = 512
RANK = 8
CELLS = WIN_LAT * WIN_LON
SLOT = 80
BANDS = LAT_CELLS // WIN_LAT
ACROSS = LON_CELLS // WIN_LON
WINDOWS = BANDS * ACROSS
EARLY = ((0, 0), (1, 0))
LATE = ((0, 1), (1, 1), (2, 0), (2, 1))
ORDER = EARLY + LATE
SPAN = 160
TOKENS = WINDOWS * SLOT
OWN = LAT_CELLS * LON_CELLS
HEAD_WIDTH = D // HEADS
GROUP = 256 // HEAD_WIDTH
GROUPS = HEADS // GROUP
STACK = GROUP * SLOT
ROW_IN, COL_IN, COR_IN = 80, 112, 32
COL_FROM, COL_PART = (16, 48, 64), 48
PACK = 2 * RANK
WIDTH = 6 * D
ROW_OUT, COL_OUT, COR_OUT = 64, 96, 32
BF16 = jnp.bfloat16
F32 = jnp.float32
VMEM_ASKED = {"send": 60, "early": 60, "late": 55, "finish": 60, "place": 55}
FIXED = ("x", "c", "gain", "qkv", "out")


def own_from(a):
    return 64 + 144 * a


def marks_at(shape, source):
    row = lax.broadcasted_iota(jnp.int32, shape, 0)
    lane = lax.broadcasted_iota(jnp.int32, shape, 1)
    return jnp.where(lane == source(row), 1.0, 0.0).astype(BF16)


def over(value, divisor):
    factor, shift = {6: (10923, 16), 12: (10923, 17), 18: (7282, 17), 24: (10923, 18)}[divisor]
    return jnp.right_shift(value * factor, shift)


def pick(test, one, other):
    return jnp.where(test, one, other)


def place_send():
    def source(row):
        at = pick(row < COL_IN, row, row - COL_IN)
        r = over(at, HALF_LON)
        ends = pick(row < COL_IN, HALF_LON * LAT_CELLS, HALF_LON * HALF_LAT)
        return pick(at < ends, LON_CELLS * r + at - HALF_LON * r, -1)

    return marks_at((COL_IN + COR_IN, OWN), source)


def place_in(window, width):
    a, b = window

    def source(cell):
        r = over(cell, WIN_LON)
        c = cell - WIN_LON * r
        row, col = WIN_LAT * a + r + HALF_LAT, WIN_LON * b + c + HALF_LON
        at = LON_CELLS * row + col - own_from(a)
        if b == ACROSS - 1:
            side = SPAN + HALF_LON * row + col - LON_CELLS - COL_FROM[a]
            corner = SPAN + COL_PART + HALF_LON * (row - LAT_CELLS) + col - LON_CELLS
            at = pick(col < LON_CELLS, at, pick(row < LAT_CELLS, side, corner))
        return pick(cell < CELLS, at, -1)

    return marks_at((SLOT, width), source)


def place_last():
    def source(row):
        rho = over(row, LON_CELLS - HALF_LON)
        j = row - (LON_CELLS - HALF_LON) * rho
        cell = WIN_LON * (HALF_LAT + rho) + j
        along = pick(j < WIN_LON, cell, cell + SLOT - WIN_LON)
        along = pick(row < (LON_CELLS - HALF_LON) * HALF_LAT, along, -1)
        at = row - ROW_OUT
        rho = over(jnp.maximum(at, 0), HALF_LON)
        corner = SLOT + WIN_LON * (HALF_LAT + rho) + HALF_LON + at - HALF_LON * rho
        corner = pick(at < HALF_LON * HALF_LAT, corner, -1)
        return pick(row < ROW_OUT, along, corner)

    return marks_at((ROW_OUT + COR_OUT, ACROSS * SLOT), source)


def place_side():
    def source(row):
        i = over(row, HALF_LON)
        a = over(i, WIN_LAT)
        cell = WIN_LON * (i - WIN_LAT * a) + HALF_LON + row - HALF_LON * i
        return pick(row < HALF_LON * (LAT_CELLS - HALF_LAT), SLOT * a + cell, -1)

    return marks_at((COL_OUT, BANDS * SLOT), source)


def place_out(at):
    def source(row):
        r = over(row, LON_CELLS)
        col = row - LON_CELLS * r
        i, j = WIN_LAT * at + r - HALF_LAT, col - HALF_LON
        late = r >= HALF_LAT
        cell = WIN_LON * pick(late, r - HALF_LAT, r + HALF_LAT) + j
        cell = pick(j < WIN_LON, cell, cell + SLOT - WIN_LON)
        inner = pick(late, SPAN + cell, cell)
        edge = 2 * SPAN + HALF_LON * i + col
        if at == 0:
            inner = pick(late, inner, (LON_CELLS - HALF_LON) * r + j)
            edge = pick(late, edge, ROW_OUT + HALF_LON * r + col)
        return pick(j < 0, edge, inner)

    return marks_at((WIN_LAT * LON_CELLS, 2 * SPAN + COL_OUT), source)


def head_marks():
    lane = lax.broadcasted_iota(jnp.int32, (16, 256), 1)
    heads = [
        jnp.where(jnp.right_shift(lane, 5) == head, 1.0, 0.0).astype(BF16)
        for head in range(GROUP)
    ]
    return jnp.stack(heads, axis=0)


def nn(left, right):
    return lax.dot_general(left, right, (((1,), (0,)), ((), ())), preferred_element_type=F32)


def nt(left, right):
    return lax.dot_general(left, right, (((1,), (1,)), ((), ())), preferred_element_type=F32)


class Staged:
    def __init__(self, names, outside, buffers, sem):
        self.copies = {x: (outside[x], buffers[x], sem[x]) for x in names if x in buffers}
        self.buffers = {x: buffers.get(x, outside[x]) for x in names}
        self.open = {}

    def fetch(self):
        for name, (ref, buffer, sem) in self.copies.items():
            self.open[name] = pltpu.make_async_copy(ref, buffer, sem)
            self.open[name].start()

    def __getitem__(self, name):
        if name in self.open:
            self.open.pop(name).wait()
        return self.buffers[name]

    def send(self, *names):
        for name in names:
            if name not in self.copies:
                continue
            ref, buffer, sem = self.copies[name]
            self.open[name] = pltpu.make_async_copy(buffer, ref, sem)
            self.open[name].start()

    def close(self):
        for name in list(self.open):
            self.open.pop(name).wait()


def call(body, ins, outs, name, scratch=(), scalars=0, near=(), flops=0):
    in_names, out_names = list(ins)[scalars:], list(outs)
    arrays = list(ins.values())
    shapes = [jax.ShapeDtypeStruct(shape, dtype) for shape, dtype in outs.values()]
    names = in_names + out_names
    far = [x for x in names if x not in near]
    kinds = dict(zip(names, arrays[scalars:] + shapes))

    def kernel(*refs):
        heads, refs = refs[:scalars], refs[scalars:]
        outside, refs = dict(zip(names, refs)), refs[len(names) :]
        buffers, refs = dict(zip(far, refs)), refs[len(far) :]
        sems, rest = refs[0], refs[1:]
        sem = {x: sems.at[at] for at, x in enumerate(far)}
        given = Staged(in_names, outside, buffers, sem)
        made = Staged(out_names, outside, buffers, sem)
        given.fetch()
        body(given, made, *heads, *rest)
        given.close()
        made.close()

    def spec(x):
        if x in near:
            return pl.BlockSpec(memory_space=pltpu.VMEM)
        return pl.BlockSpec(memory_space=pltpu.HBM if x in FIXED else pl.ANY)

    return pl.pallas_call(
        kernel,
        out_shape=shapes,
        in_specs=[pl.BlockSpec(memory_space=pltpu.SMEM)] * scalars + [spec(x) for x in in_names],
        out_specs=[spec(x) for x in out_names],
        scratch_shapes=[pltpu.VMEM(kinds[x].shape, kinds[x].dtype) for x in far]
        + [pltpu.SemaphoreType.DMA((max(len(far), 1),))]
        + list(scratch),
        compiler_params=pltpu.CompilerParams(vmem_limit_bytes=VMEM_ASKED[name] << 20),
        cost_estimate=pl.CostEstimate(
            flops=flops, bytes_accessed=4 * 1024 * 1024, transcendentals=0
        ),
        name=name,
    )(*arrays)


def send_body(given, made):
    place = place_send()
    for at, name in enumerate(("x", "c")):
        ref = given[name]
        made["row"][ROW_IN * at : ROW_IN * (at + 1)] = ref[:ROW_IN]
        picked = nn(place, ref[...]).astype(BF16)
        made["col"][COL_IN * at : COL_IN * (at + 1)] = picked[:COL_IN]
        made["cor"][COR_IN * at : COR_IN * (at + 1)] = picked[COL_IN:]
    made.send("col", "row", "cor")


def split_heads(block, marks):
    tiles = block.reshape(1, SLOT // 16, 16, 256) * marks[:, None]
    return tiles.reshape(STACK, 256)


def join_heads(stacked):
    lane = lax.broadcasted_iota(jnp.int32, (SLOT, 128), 1)
    parts = [stacked[SLOT * h : SLOT * (h + 1)] for h in range(4)]
    low = jnp.where(lane < 32, parts[0], parts[1])
    high = jnp.where(lane < 96, parts[2], parts[3])
    return jnp.where(lane < 64, low, high)


def per_query(weights, block):
    turned = weights.T
    half = STACK // 2
    return jnp.concatenate(
        (
            join_heads(nn(turned[:half], block[:, :128])),
            join_heads(nn(turned[half:], block[:, 128:])),
        ),
        axis=1,
    )


def adapters(pack_ref):
    return (
        pack_ref[:, :D],
        pack_ref[:, D : 4 * D],
        pack_ref[:, 4 * D : 5 * D],
        pack_ref[:, 5 * D :],
    )


def attend(given, made, windows, blocks, pole, hidden, packed, bblend, marks_ref):
    count = len(windows)
    for first in range(0, count, 2):
        rows = pl.ds(SLOT * first, 2 * SLOT)
        for at, (source, into) in enumerate((("x", "xw"), ("c", "cw"))):
            blocks(given, made, source, at, into, first)
        wide = made["xw"][rows].astype(F32)
        center = wide - jnp.mean(wide, axis=-1, keepdims=True)
        spread = jnp.mean(center * center, axis=-1, keepdims=True)
        normed = (center * lax.rsqrt(spread + 1e-05) * given["gain"][...]).astype(BF16)
        hidden[rows] = normed
        down, up, odown, oup = adapters(given["pack"])
        low = nt(normed, down).astype(BF16)
        packed[rows] = (nn(normed, given["qkv"][...]) + nn(low, up)).astype(BF16)
        cot = made["cw"][rows]
        back_low = nt(cot, oup).astype(BF16)
        bblend[rows] = (nt(cot, given["out"][...]) + nn(back_low, odown)).astype(BF16)
    made.send("xw", "cw")

    marks_ref[...] = head_marks()
    blended_ref, back_ref = made["blended"], made["back"]
    rest = jnp.zeros((SLOT - CELLS, STACK), F32)
    scale = 1.0 / math.sqrt(HEAD_WIDTH)
    if pole is not None:
        key_late = lax.broadcasted_iota(jnp.int32, (CELLS, STACK), 0) >= CELLS // 2
        query_at = lax.rem(lax.broadcasted_iota(jnp.int32, (CELLS, STACK), 1), SLOT)
        apart = (key_late != (query_at >= CELLS // 2)).astype(F32) * -1e30

    def one_window(w, carry):
        rows = pl.ds(pl.multiple_of(w * SLOT, SLOT), SLOT)
        marks = marks_ref[...]
        for g in range(GROUPS):
            at = 256 * g
            query = packed[rows, at : at + 256]
            key = packed[rows, D + at : D + at + 256]
            value = packed[rows, 2 * D + at : 2 * D + at + 256]
            back = bblend[rows, at : at + 256]
            queries = split_heads(query, marks)
            backs = split_heads(back, marks)
            scores = nt(key, queries)[:CELLS] * scale
            if pole is not None:
                late = w >= sum(a < BANDS - 1 for a, _ in windows)
                scores = scores + apart * jnp.where(jnp.logical_and(pole > 0, late), 1.0, 0.0)
            top = jnp.max(scores, axis=0, keepdims=True)
            exponent = jnp.exp(scores - top)
            weights = exponent * (1.0 / jnp.sum(exponent, axis=0, keepdims=True))
            rounded = jnp.concatenate((weights, rest), axis=0).astype(BF16)
            blended_ref[rows, at : at + 256] = per_query(rounded, value).astype(BF16)
            back_weights = nt(value, backs)[:CELLS].astype(BF16).astype(F32)
            product = weights * back_weights
            total = jnp.sum(product, axis=0, keepdims=True)
            back_scores = (product - weights * total) * scale
            back_scores = jnp.concatenate((back_scores, rest), axis=0).astype(BF16)
            back_ref[rows, at : at + 256] = per_query(back_scores, key).astype(BF16)
            back_ref[rows, D + at : D + at + 256] = nn(back_scores, queries).astype(BF16)
            back_ref[rows, 2 * D + at : 2 * D + at + 256] = nn(rounded, backs).astype(BF16)
        return carry

    lax.fori_loop(0, count, one_window, 0, unroll=2)
    made.send("blended", "back")

    down, up, odown, oup = adapters(given["pack"])
    cot = made.buffers["cw"][...]
    blended = blended_ref[...]
    back = back_ref[...]
    return jnp.concatenate(
        (
            nn(nt(up, back).astype(BF16), hidden[...])[:RANK],
            nn(nt(down, hidden[...]).astype(BF16), back)[:RANK],
            nn(nt(oup, cot).astype(BF16), blended)[:RANK],
            nn(nt(odown, blended).astype(BF16), cot)[:RANK],
        ),
        axis=1,
    )


def early_blocks(given, made, source, at, into, first):
    for k in range(first, first + 2):
        begin = own_from(EARLY[k][0])
        own = given[source][begin : begin + SPAN]
        place = place_in(EARLY[k], SPAN)
        made[into][SLOT * k : SLOT * (k + 1)] = nn(place, own).astype(BF16)


def late_blocks(given, made, source, at, into, first):
    for k in range(first, first + 2):
        a, b = LATE[k]
        ref = given[source]
        begin = own_from(a)
        if a < BANDS - 1:
            own = ref[begin : begin + SPAN]
        else:
            row = given["row"][ROW_IN * at : ROW_IN * (at + 1)]
            own = jnp.concatenate((ref[begin:], row), axis=0)
        side = given["col"][pl.ds(COL_IN * at + COL_FROM[a], COL_PART)]
        corner = given["cor"][COR_IN * at : COR_IN * (at + 1)]
        block = jnp.concatenate((own, side, corner), axis=0)
        place = place_in(LATE[k], SPAN + COL_PART + COR_IN)
        made[into][SLOT * k : SLOT * (k + 1)] = nn(place, block).astype(BF16)


def early_body(given, made, *scratch):
    grads = attend(given, made, EARLY, early_blocks, None, *scratch)
    made["grads"][...] = grads
    made.send("grads")


def late_body(given, made, pole_ref, *scratch):
    grads = attend(given, made, LATE, late_blocks, pole_ref[0], *scratch)
    grads = grads + given["grads"][...]
    tiles = made["tiles"]
    for owner in range(16):
        at = 256 * owner
        if at < WIDTH:
            both = (grads[:, at : at + 128], grads[:, at + 128 : at + 256])
            tiles[owner] = jnp.concatenate(both, axis=0).astype(BF16)
        else:
            tiles[owner] = jnp.zeros((16, 128), BF16)
    made.send("tiles")


def finish_body(given, made):
    down, up, odown, oup = adapters(given["pack"])
    for part, first, count in (("1", 0, 1), ("2", 1, 2)):
        for k in range(count):
            rows = pl.ds(2 * SLOT * k, 2 * SLOT)
            into = pl.ds(2 * SLOT * (first + k), 2 * SLOT)
            wide = given["xw" + part][rows].astype(F32)
            blended = given["blended" + part][rows]
            low = nt(blended, odown).astype(BF16)
            update = (nn(blended, given["out"][...]) + nn(low, oup)).astype(BF16)
            made["mixed"][into] = (wide + update.astype(F32)).astype(BF16)
            back = given["back" + part][rows]
            back_low = nt(back, up).astype(BF16)
            back_hidden = nt(back, given["qkv"][...]) + nn(back_low, down)
            center = wide - jnp.mean(wide, axis=-1, keepdims=True)
            spread = jnp.mean(center * center, axis=-1, keepdims=True)
            inverse = lax.rsqrt(spread + 1e-05)
            normed = center * inverse
            scaled = back_hidden * given["gain"][...]
            along = jnp.mean(scaled * normed, axis=-1, keepdims=True)
            tokens = scaled - jnp.mean(scaled, axis=-1, keepdims=True) - normed * along
            tokens = (inverse * tokens).astype(BF16).astype(F32)
            cot = given["cw" + part][rows].astype(F32)
            made["grad"][into] = (cot + tokens).astype(BF16)
    last, side_place = place_last(), place_side()
    for at, name in enumerate(("mixed", "grad")):
        ref = made[name]
        ends = nn(last, ref[SLOT * 4 :]).astype(BF16)
        made["row"][ROW_OUT * at : ROW_OUT * (at + 1)] = ends[:ROW_OUT]
        made["cor"][COR_OUT * at : COR_OUT * (at + 1)] = ends[ROW_OUT:]
        ends = [ref[SLOT * k : SLOT * (k + 1)] for k in (2, 3, 5)]
        side = nn(side_place, jnp.concatenate(ends, axis=0)).astype(BF16)
        made["col"][COL_OUT * at : COL_OUT * (at + 1)] = side
    made.send("col", "row", "cor", "mixed", "grad")


def place_body(given, made):
    rows = WIN_LAT * LON_CELLS
    places = [place_out(a) for a in range(BANDS)]
    for at, name in enumerate(("mixed", "grad")):
        ref = given[name]

        def band(a):
            slots = [ORDER.index((a, b)) for b in range(ACROSS)]
            return [ref[SLOT * k : SLOT * (k + 1)] for k in slots]

        for a in range(BANDS):
            if a:
                before = band(a - 1)
            else:
                before = [
                    given["row"][ROW_OUT * at : ROW_OUT * (at + 1)],
                    given["cor"][COR_OUT * at : COR_OUT * (at + 1)],
                    ref[: SPAN - ROW_OUT - COR_OUT],
                ]
            side = given["col"][COL_OUT * at : COL_OUT * (at + 1)]
            source = jnp.concatenate((*before, *band(a), side), axis=0)
            out = made["all_" + name]
            out[rows * a : rows * (a + 1)] = nn(places[a], source).astype(BF16)
        made.send("all_" + name)


def grads_kernel(scale, tiles_ref, *outs):
    tile = 0
    for ref in outs:
        for at in range(ref.shape[1] // 128):
            both = tiles_ref[tile // 2].astype(F32) * scale
            part = both[8 * (tile % 2) : 8 * (tile % 2) + 8]
            ref[:, 128 * at : 128 * (at + 1)] = part
            tile += 1


def exchange(tiles, axis):
    return lax.all_to_all(tiles, axis, 0, 0, tiled=True)


def sum_tiles(tiles):
    return jnp.sum(tiles.astype(F32), axis=0).astype(BF16)


def gather_tiles(tile, axis):
    spread = jnp.broadcast_to(tile[None], (lax.axis_size(axis),) + tile.shape)
    return exchange(spread, axis)


def start_total(tiles):
    return exchange(tiles, "lat")


def total_over_mesh(own):
    own = sum_tiles(gather_tiles(sum_tiles(own), "lon"))
    return gather_tiles(own, "lat")


def moved(block, lat_step, lon_step):
    lats, lons = lax.axis_size("lat"), lax.axis_size("lon")
    if lat_step == 0:
        return lax.ppermute(block, "lon", [(i, (i + lon_step) % lons) for i in range(lons)])
    if lon_step == 0:
        return lax.ppermute(block, "lat", [(i, (i + lat_step) % lats) for i in range(lats)])
    route = [
        (i * lons + j, (i + lat_step) % lats * lons + (j + lon_step) % lons)
        for i in range(lats)
        for j in range(lons)
    ]
    return lax.ppermute(block, ("lat", "lon"), route)


def attended(count, last):
    outs = {
        "xw": ((SLOT * count, D), BF16),
        "cw": ((SLOT * count, D), BF16),
        "blended": ((SLOT * count, D), BF16),
        "back": ((SLOT * count, 3 * D), BF16),
    }
    outs.update(last)
    scratch = [
        pltpu.VMEM((SLOT * count, D), BF16),
        pltpu.VMEM((SLOT * count, 3 * D), BF16),
        pltpu.VMEM((SLOT * count, D), BF16),
        pltpu.VMEM((GROUP, 16, 256), BF16),
    ]
    return outs, scratch


def shards(
    fine_tokens, cotangent, norm_gain, qkv_weight, qkv_down, qkv_up, out_weight, out_down, out_up
):
    lats, lons = lax.axis_size("lat"), lax.axis_size("lon")
    tokens = fine_tokens.reshape(OWN, D)
    cots = cotangent.reshape(OWN, D)
    pack = jnp.concatenate((qkv_down.T, qkv_up, out_down.T, out_up), axis=1)
    pack = jnp.pad(pack, ((0, PACK - RANK), (0, 0)))
    weights = {
        "gain": norm_gain.reshape(1, D),
        "pack": pack,
        "qkv": qkv_weight,
        "out": out_weight,
    }
    pole = (lax.axis_index("lat") == lats - 1).astype(jnp.int32).reshape(1)
    row, col, cor = call(
        send_body,
        {"x": tokens, "c": cots},
        {
            "row": ((2 * ROW_IN, D), BF16),
            "col": ((2 * COL_IN, D), BF16),
            "cor": ((2 * COR_IN, D), BF16),
        },
        "send",
        near=("row", "col", "cor"),
        flops=10**8,
    )
    col = moved(col, 0, -1)
    row = moved(row, -1, 0)
    cor = moved(cor, -1, -1)
    outs, scratch = attended(len(EARLY), {"grads": ((RANK, WIDTH), F32)})
    xw1, cw1, blended1, back1, grads = call(
        early_body,
        {"x": tokens, "c": cots, **weights},
        outs,
        "early",
        scratch=scratch,
        flops=4 * 10**9,
    )
    outs, scratch = attended(len(LATE), {"tiles": ((16, 16, 128), BF16)})
    xw2, cw2, blended2, back2, tiles = call(
        late_body,
        {
            "pole": pole,
            "x": tokens,
            "col": col,
            "row": row,
            "cor": cor,
            "c": cots,
            **weights,
            "grads": grads,
        },
        outs,
        "late",
        scratch=scratch,
        scalars=1,
        near=("row", "col", "cor", "tiles"),
        flops=8 * 10**9,
    )
    own = start_total(tiles)
    mixed, grad, row, col, cor = call(
        finish_body,
        {
            "xw1": xw1,
            "blended1": blended1,
            "pack": pack,
            "out": out_weight,
            "back1": back1,
            "qkv": qkv_weight,
            "gain": weights["gain"],
            "cw1": cw1,
            "xw2": xw2,
            "blended2": blended2,
            "back2": back2,
            "cw2": cw2,
        },
        {
            "mixed": ((TOKENS, D), BF16),
            "grad": ((TOKENS, D), BF16),
            "row": ((2 * ROW_OUT, D), BF16),
            "col": ((2 * COL_OUT, D), BF16),
            "cor": ((2 * COR_OUT, D), BF16),
        },
        "finish",
        near=("row", "col", "cor"),
        flops=3 * 10**9,
    )
    own, mixed, grad, row, col, cor = lax.optimization_barrier((own, mixed, grad, row, col, cor))
    col = moved(col, 0, 1)
    row = moved(row, 1, 0)
    cor = moved(cor, 1, 1)
    tiles = total_over_mesh(own)
    mixed, grad = call(
        place_body,
        {"mixed": mixed, "row": row, "cor": cor, "col": col, "grad": grad},
        {"all_mixed": ((OWN, D), BF16), "all_grad": ((OWN, D), BF16)},
        "place",
        near=("row", "col", "cor"),
        flops=10**9,
    )
    scale = 1.0 / math.sqrt(OWN * lats * lons)

    def last_grads(*refs):
        grads_kernel(scale, *refs)

    grads = pl.pallas_call(
        last_grads,
        out_shape=[
            jax.ShapeDtypeStruct((RANK, D), F32),
            jax.ShapeDtypeStruct((RANK, 3 * D), F32),
            jax.ShapeDtypeStruct((RANK, D), F32),
            jax.ShapeDtypeStruct((RANK, D), F32),
        ],
        name="grads",
    )(tiles)
    shape = (LAT_CELLS, LON_CELLS, D)
    return (
        mixed.reshape(shape),
        grad.reshape(shape),
        grads[0].T,
        grads[1],
        grads[2].T,
        grads[3],
    )


def solution(mesh):
    in_specs = (P("lat", "lon", None), P("lat", "lon", None), P(), P(), P(), P(), P(), P(), P())
    out_specs = (P("lat", "lon", None), P("lat", "lon", None), P(), P(), P(), P())
    return jax.shard_map(shards, mesh=mesh, in_specs=in_specs, out_specs=out_specs, check_vma=False)
```

```python
import math

import jax
import jax.numpy as jnp
from jax import lax
from jax.experimental import pallas as pl
from jax.experimental.pallas import tpu as pltpu
from jax.sharding import PartitionSpec as P

HEADS = 16
WIN_LAT = 6
WIN_LON = 12
HALF_LAT = WIN_LAT // 2
HALF_LON = WIN_LON // 2
LAT_CELLS = 18
LON_CELLS = 24
D = 512
RANK = 8
CELLS = WIN_LAT * WIN_LON
SLOT = 80
BANDS = LAT_CELLS // WIN_LAT
ACROSS = LON_CELLS // WIN_LON
WINDOWS = BANDS * ACROSS
EARLY = ((0, 0), (1, 0))
LATE = ((0, 1), (1, 1), (2, 0), (2, 1))
ORDER = EARLY + LATE
SPAN = 160
TOKENS = WINDOWS * SLOT
OWN = LAT_CELLS * LON_CELLS
HEAD_WIDTH = D // HEADS
GROUP = 256 // HEAD_WIDTH
GROUPS = HEADS // GROUP
STACK = GROUP * SLOT
ROW_IN, COL_IN, COR_IN = 80, 112, 32
COL_FROM, COL_PART = (16, 48, 64), 48
WIDTH = 6 * D
ROW_OUT, COL_OUT, COR_OUT = 64, 96, 32
BF16 = jnp.bfloat16
F32 = jnp.float32
VMEM_ASKED = {"send": 60, "early": 53, "late": 52, "finish": 50, "place": 52, "grads": 52}
GRADS = ("qkv_down", "qkv_up", "out_down", "out_up")
FIXED = ("x", "c", "gain", "qkv", "out", "xw", "cw", "blended", "back", "mixed", "grad", "xw1", "xw2", "cw1", "cw2", "blended1", "blended2", "back1", "back2")


def own_from(a):
    return 64 + 144 * a


def marks_at(shape, source):
    row = lax.broadcasted_iota(jnp.int32, shape, 0)
    lane = lax.broadcasted_iota(jnp.int32, shape, 1)
    return jnp.where(lane == source(row), 1.0, 0.0).astype(BF16)


def over(value, divisor):
    factor, shift = {6: (10923, 16), 12: (10923, 17), 18: (7282, 17), 24: (10923, 18)}[divisor]
    return jnp.right_shift(value * factor, shift)


def pick(test, one, other):
    return jnp.where(test, one, other)


def place_send():
    def source(row):
        at = pick(row < COL_IN, row, row - COL_IN)
        r = over(at, HALF_LON)
        ends = pick(row < COL_IN, HALF_LON * LAT_CELLS, HALF_LON * HALF_LAT)
        return pick(at < ends, LON_CELLS * r + at - HALF_LON * r, -1)

    return marks_at((COL_IN + COR_IN, OWN), source)


def place_in(window, width):
    a, b = window

    def source(cell):
        r = over(cell, WIN_LON)
        c = cell - WIN_LON * r
        row, col = WIN_LAT * a + r + HALF_LAT, WIN_LON * b + c + HALF_LON
        at = LON_CELLS * row + col - own_from(a)
        if b == ACROSS - 1:
            side = SPAN + HALF_LON * row + col - LON_CELLS - COL_FROM[a]
            corner = SPAN + COL_PART + HALF_LON * (row - LAT_CELLS) + col - LON_CELLS
            at = pick(col < LON_CELLS, at, pick(row < LAT_CELLS, side, corner))
        return pick(cell < CELLS, at, -1)

    return marks_at((SLOT, width), source)


def place_last():
    def source(row):
        rho = over(row, LON_CELLS - HALF_LON)
        j = row - (LON_CELLS - HALF_LON) * rho
        cell = WIN_LON * (HALF_LAT + rho) + j
        along = pick(j < WIN_LON, cell, cell + SLOT - WIN_LON)
        along = pick(row < (LON_CELLS - HALF_LON) * HALF_LAT, along, -1)
        at = row - ROW_OUT
        rho = over(jnp.maximum(at, 0), HALF_LON)
        corner = SLOT + WIN_LON * (HALF_LAT + rho) + HALF_LON + at - HALF_LON * rho
        corner = pick(at < HALF_LON * HALF_LAT, corner, -1)
        return pick(row < ROW_OUT, along, corner)

    return marks_at((ROW_OUT + COR_OUT, ACROSS * SLOT), source)


def place_side():
    def source(row):
        i = over(row, HALF_LON)
        a = over(i, WIN_LAT)
        cell = WIN_LON * (i - WIN_LAT * a) + HALF_LON + row - HALF_LON * i
        return pick(row < HALF_LON * (LAT_CELLS - HALF_LAT), SLOT * a + cell, -1)

    return marks_at((COL_OUT, BANDS * SLOT), source)


def place_out(at):
    def source(row):
        r = over(row, LON_CELLS)
        col = row - LON_CELLS * r
        i, j = WIN_LAT * at + r - HALF_LAT, col - HALF_LON
        late = r >= HALF_LAT
        cell = WIN_LON * pick(late, r - HALF_LAT, r + HALF_LAT) + j
        cell = pick(j < WIN_LON, cell, cell + SLOT - WIN_LON)
        inner = pick(late, SPAN + cell, cell)
        edge = 2 * SPAN + HALF_LON * i + col
        if at == 0:
            inner = pick(late, inner, (LON_CELLS - HALF_LON) * r + j)
            edge = pick(late, edge, ROW_OUT + HALF_LON * r + col)
        return pick(j < 0, edge, inner)

    return marks_at((WIN_LAT * LON_CELLS, 2 * SPAN + COL_OUT), source)


def head_marks():
    lane = lax.broadcasted_iota(jnp.int32, (16, 256), 1)
    heads = [
        jnp.where(jnp.right_shift(lane, 5) == head, 1.0, 0.0).astype(BF16)
        for head in range(GROUP)
    ]
    return jnp.stack(heads, axis=0)


def nn(left, right):
    return lax.dot_general(left, right, (((1,), (0,)), ((), ())), preferred_element_type=F32)


def nt(left, right):
    return lax.dot_general(left, right, (((1,), (1,)), ((), ())), preferred_element_type=F32)


class Staged:
    def __init__(self, names, outside, buffers, sem):
        self.copies = {x: (outside[x], buffers[x], sem[x]) for x in names if x in buffers}
        self.buffers = {x: buffers.get(x, outside[x]) for x in names}
        self.open = {}

    def fetch(self, names):
        for name in names:
            if name not in self.copies:
                continue
            ref, buffer, sem = self.copies[name]
            self.open[name] = pltpu.make_async_copy(ref, buffer, sem)
            self.open[name].start()

    def __getitem__(self, name):
        if name in self.open:
            self.open.pop(name).wait()
        return self.buffers[name]

    def send(self, *names):
        for name in names:
            if name not in self.copies:
                continue
            ref, buffer, sem = self.copies[name]
            self.open[name] = pltpu.make_async_copy(buffer, ref, sem)
            self.open[name].start()

    def close(self):
        for name in list(self.open):
            self.open.pop(name).wait()


def call(body, ins, outs, name, scratch=(), scalars=0, near=(), keep=(), first=(), flops=0):
    arrays = list(ins.values())
    outs = dict(outs, **{x + "_kept": (ins[x].shape, ins[x].dtype) for x in keep})
    in_names, out_names = list(ins)[scalars:], list(outs)
    near = (*near, *(x + "_kept" for x in keep))
    shapes = [jax.ShapeDtypeStruct(shape, dtype) for shape, dtype in outs.values()]
    names = in_names + out_names
    far = [x for x in names if x not in near]
    own = [x for x in far if x not in keep]
    kinds = dict(zip(names, arrays[scalars:] + shapes))

    def kernel(*refs):
        heads, refs = refs[:scalars], refs[scalars:]
        outside, refs = dict(zip(names, refs)), refs[len(names) :]
        buffers, refs = dict(zip(own, refs)), refs[len(own) :]
        buffers.update({x: outside[x + "_kept"] for x in keep})
        sems, rest = refs[0], refs[1:]
        sem = {x: sems.at[at] for at, x in enumerate(far)}
        given = Staged(in_names, outside, buffers, sem)
        made = Staged(out_names, outside, buffers, sem)
        given.fetch(first or list(ins)[scalars:])
        body(given, made, *heads, *rest)
        given.close()
        made.close()

    def spec(x):
        if x in near:
            return pl.BlockSpec(memory_space=pltpu.VMEM)
        return pl.BlockSpec(memory_space=pltpu.HBM if x in FIXED else pl.ANY)

    return pl.pallas_call(
        kernel,
        out_shape=shapes,
        in_specs=[pl.BlockSpec(memory_space=pltpu.SMEM)] * scalars + [spec(x) for x in in_names],
        out_specs=[spec(x) for x in out_names],
        scratch_shapes=[pltpu.VMEM(kinds[x].shape, kinds[x].dtype) for x in own]
        + [pltpu.SemaphoreType.DMA((max(len(far), 1),))]
        + list(scratch),
        compiler_params=pltpu.CompilerParams(vmem_limit_bytes=VMEM_ASKED[name] << 20),
        cost_estimate=pl.CostEstimate(
            flops=flops, bytes_accessed=4 * 1024 * 1024, transcendentals=0
        ),
        name=name,
    )(*arrays)


def send_body(given, made):
    place = place_send()
    for at, name in enumerate(("x", "c")):
        ref = given[name]
        made["row"][ROW_IN * at : ROW_IN * (at + 1)] = ref[:ROW_IN]
        picked = nn(place, ref[...]).astype(BF16)
        made["col"][COL_IN * at : COL_IN * (at + 1)] = picked[:COL_IN]
        made["cor"][COR_IN * at : COR_IN * (at + 1)] = picked[COL_IN:]
    made.send("col", "row", "cor")


def split_heads(block, marks):
    tiles = block.reshape(1, SLOT // 16, 16, 256) * marks[:, None]
    return tiles.reshape(STACK, 256)


def join_heads(stacked):
    lane = lax.broadcasted_iota(jnp.int32, (SLOT, 128), 1)
    parts = [stacked[SLOT * h : SLOT * (h + 1)] for h in range(4)]
    low = jnp.where(lane < 32, parts[0], parts[1])
    high = jnp.where(lane < 96, parts[2], parts[3])
    return jnp.where(lane < 64, low, high)


def per_query(weights, block):
    turned = weights.T
    half = STACK // 2
    return jnp.concatenate(
        (
            join_heads(nn(turned[:half], block[:, :128])),
            join_heads(nn(turned[half:], block[:, 128:])),
        ),
        axis=1,
    )


def adapters(pack_ref):
    wide = pack_ref[:, :WIDTH]
    factors = jnp.concatenate((wide, jnp.zeros_like(wide)), axis=0).astype(BF16)
    cuts = (0, D, 4 * D, 5 * D, WIDTH)
    return *(factors[:, a:b] for a, b in zip(cuts, cuts[1:])), pack_ref[:1, WIDTH:]


def attend(given, made, windows, blocks, pole, hidden, packed, bblend, marks_ref):
    count = len(windows)
    for first in range(0, count, 2):
        rows = pl.ds(SLOT * first, 2 * SLOT)
        blocks(given, made, "x", 0, "xw", first)
        if first == 0:
            given.fetch(("qkv", "c", "out"))
            down, up, odown, oup, gain = adapters(given["pack"])
        wide = made["xw"][rows].astype(F32)
        center = wide - jnp.mean(wide, axis=-1, keepdims=True)
        spread = jnp.mean(center * center, axis=-1, keepdims=True)
        normed = (center * lax.rsqrt(spread + 1e-05) * gain).astype(BF16)
        hidden[rows] = normed
        low = nt(normed, down).astype(BF16)
        packed[rows] = (nn(normed, given["qkv"][...]) + nn(low, up)).astype(BF16)
        blocks(given, made, "c", 1, "cw", first)
        cot = made["cw"][rows]
        back_low = nt(cot, oup).astype(BF16)
        bblend[rows] = (nt(cot, given["out"][...]) + nn(back_low, odown)).astype(BF16)
    made.send("xw", "cw")

    marks_ref[...] = head_marks()
    blended_ref, back_ref = made["blended"], made["back"]
    rest = jnp.zeros((SLOT - CELLS, STACK), F32)
    scale = 1.0 / math.sqrt(HEAD_WIDTH)
    if pole is not None:
        key_late = lax.broadcasted_iota(jnp.int32, (CELLS, STACK), 0) >= CELLS // 2
        query_at = lax.rem(lax.broadcasted_iota(jnp.int32, (CELLS, STACK), 1), SLOT)
        apart = (key_late != (query_at >= CELLS // 2)).astype(F32) * -1e30

    def one_window(w, carry):
        rows = pl.ds(pl.multiple_of(w * SLOT, SLOT), SLOT)
        marks = marks_ref[...]
        for g in range(GROUPS):
            at = 256 * g
            query = packed[rows, at : at + 256]
            key = packed[rows, D + at : D + at + 256]
            value = packed[rows, 2 * D + at : 2 * D + at + 256]
            back = bblend[rows, at : at + 256]
            queries = split_heads(query, marks)
            backs = split_heads(back, marks)
            scores = nt(key, queries)[:CELLS] * scale
            if pole is not None:
                late = w >= sum(a < BANDS - 1 for a, _ in windows)
                scores = scores + apart * jnp.where(jnp.logical_and(pole > 0, late), 1.0, 0.0)
            top = jnp.max(scores, axis=0, keepdims=True)
            exponent = jnp.exp(scores - top)
            weights = exponent * (1.0 / jnp.sum(exponent, axis=0, keepdims=True))
            rounded = jnp.concatenate((weights, rest), axis=0).astype(BF16)
            blended_ref[rows, at : at + 256] = per_query(rounded, value).astype(BF16)
            back_weights = nt(value, backs)[:CELLS].astype(BF16).astype(F32)
            product = weights * back_weights
            total = jnp.sum(product, axis=0, keepdims=True)
            back_scores = (product - weights * total) * scale
            back_scores = jnp.concatenate((back_scores, rest), axis=0).astype(BF16)
            back_ref[rows, at : at + 256] = per_query(back_scores, key).astype(BF16)
            back_ref[rows, D + at : D + at + 256] = nn(back_scores, queries).astype(BF16)
            back_ref[rows, 2 * D + at : 2 * D + at + 256] = nn(rounded, backs).astype(BF16)
        return carry

    lax.fori_loop(0, count, one_window, 0, unroll=2)
    made.send("blended", "back")

    cot = made.buffers["cw"][...]
    blended = blended_ref[...]
    back = back_ref[...]
    return jnp.concatenate(
        (
            nn(nt(up, back).astype(BF16), hidden[...])[:RANK],
            nn(nt(down, hidden[...]).astype(BF16), back)[:RANK],
            nn(nt(oup, cot).astype(BF16), blended)[:RANK],
            nn(nt(odown, blended).astype(BF16), cot)[:RANK],
        ),
        axis=1,
    )


def early_blocks(given, made, source, at, into, first):
    for k in range(first, first + 2):
        begin = own_from(EARLY[k][0])
        own = given[source][begin : begin + SPAN]
        place = place_in(EARLY[k], SPAN)
        made[into][SLOT * k : SLOT * (k + 1)] = nn(place, own).astype(BF16)


def late_blocks(given, made, source, at, into, first):
    for k in range(first, first + 2):
        a, b = LATE[k]
        ref = given[source]
        begin = own_from(a)
        if a < BANDS - 1:
            own = ref[begin : begin + SPAN]
        else:
            row = given["row_in"][ROW_IN * at : ROW_IN * (at + 1)]
            own = jnp.concatenate((ref[begin:], row), axis=0)
        side = given["col_in"][pl.ds(COL_IN * at + COL_FROM[a], COL_PART)]
        corner = given["cor_in"][COR_IN * at : COR_IN * (at + 1)]
        block = jnp.concatenate((own, side, corner), axis=0)
        place = place_in(LATE[k], SPAN + COL_PART + COR_IN)
        made[into][SLOT * k : SLOT * (k + 1)] = nn(place, block).astype(BF16)


def early_body(given, made, *scratch):
    grads = attend(given, made, EARLY, early_blocks, None, *scratch)
    made["grads"][...] = grads
    made.send("grads")


def late_body(given, made, pole_ref, *scratch):
    grads = attend(given, made, LATE, late_blocks, pole_ref[0], *scratch)
    grads = grads + given["grads"][...]
    tiles = made["tiles"]
    for owner in range(16):
        at = 256 * owner
        if at < WIDTH:
            both = (grads[:, at : at + 128], grads[:, at + 128 : at + 256])
            tiles[owner] = jnp.concatenate(both, axis=0).astype(BF16)
        else:
            tiles[owner] = jnp.zeros((16, 128), BF16)
    made.send("tiles")


def finish_body(given, made):
    parts = (("1", 0, 1), ("2", 1, 2))
    given["xw1"], given["blended1"], given["out"]
    given.fetch(("xw2", "blended2", "qkv", "back1", "cw1"))
    down, up, odown, oup, gain = adapters(given["pack"])
    for part, first, count in parts:
        for k in range(count):
            rows = pl.ds(2 * SLOT * k, 2 * SLOT)
            into = pl.ds(2 * SLOT * (first + k), 2 * SLOT)
            wide = given["xw" + part][rows].astype(F32)
            blended = given["blended" + part][rows]
            low = nt(blended, odown).astype(BF16)
            update = (nn(blended, given["out"][...]) + nn(low, oup)).astype(BF16)
            made["mixed"][into] = (wide + update.astype(F32)).astype(BF16)
    given.fetch(("back2", "cw2"))
    made.send("mixed")
    for part, first, count in parts:
        for k in range(count):
            rows = pl.ds(2 * SLOT * k, 2 * SLOT)
            into = pl.ds(2 * SLOT * (first + k), 2 * SLOT)
            wide = given["xw" + part][rows].astype(F32)
            back = given["back" + part][rows]
            back_low = nt(back, up).astype(BF16)
            back_hidden = nt(back, given["qkv"][...]) + nn(back_low, down)
            center = wide - jnp.mean(wide, axis=-1, keepdims=True)
            spread = jnp.mean(center * center, axis=-1, keepdims=True)
            inverse = lax.rsqrt(spread + 1e-05)
            normed = center * inverse
            scaled = back_hidden * gain
            along = jnp.mean(scaled * normed, axis=-1, keepdims=True)
            tokens = scaled - jnp.mean(scaled, axis=-1, keepdims=True) - normed * along
            tokens = (inverse * tokens).astype(BF16).astype(F32)
            cot = given["cw" + part][rows].astype(F32)
            made["grad"][into] = (cot + tokens).astype(BF16)
    made.send("grad")
    last, side_place = place_last(), place_side()
    for at, name in enumerate(("mixed", "grad")):
        ref = made.buffers[name]
        ends = nn(last, ref[SLOT * 4 :]).astype(BF16)
        made["row"][ROW_OUT * at : ROW_OUT * (at + 1)] = ends[:ROW_OUT]
        made["cor"][COR_OUT * at : COR_OUT * (at + 1)] = ends[ROW_OUT:]
        ends = [ref[SLOT * k : SLOT * (k + 1)] for k in (2, 3, 5)]
        side = nn(side_place, jnp.concatenate(ends, axis=0)).astype(BF16)
        made["col"][COL_OUT * at : COL_OUT * (at + 1)] = side
    made.send("col", "row", "cor")


def place_body(given, made):
    rows = WIN_LAT * LON_CELLS
    places = [place_out(a) for a in range(BANDS)]
    for at, name in enumerate(("mixed", "grad")):
        ref = given[name]

        def band(a):
            slots = [ORDER.index((a, b)) for b in range(ACROSS)]
            return [ref[SLOT * k : SLOT * (k + 1)] for k in slots]

        for a in range(BANDS):
            if a:
                before = band(a - 1)
            else:
                before = [
                    given["row"][ROW_OUT * at : ROW_OUT * (at + 1)],
                    given["cor"][COR_OUT * at : COR_OUT * (at + 1)],
                    ref[: SPAN - ROW_OUT - COR_OUT],
                ]
            side = given["col"][COL_OUT * at : COL_OUT * (at + 1)]
            source = jnp.concatenate((*before, *band(a), side), axis=0)
            out = made["all_" + name]
            out[rows * a : rows * (a + 1)] = nn(places[a], source).astype(BF16)
        made.send("all_" + name)


def grads_body(scale, given, made):
    tile = 0
    for name in GRADS:
        ref = made[name]
        for at in range(ref.shape[1] // 128):
            owner, row = tile // 2, RANK * (tile % 2)
            wide = given["tiles"][owner].astype(F32) * scale
            ref[:, 128 * at : 128 * (at + 1)] = wide[row : row + RANK]
            tile += 1
    made.send(*GRADS)


def exchange(tiles, axis):
    return lax.all_to_all(tiles, axis, 0, 0, tiled=True)


def sum_tiles(tiles):
    return jnp.sum(tiles.astype(F32), axis=0).astype(BF16)


def gather_tiles(tile, axis):
    spread = jnp.broadcast_to(tile[None], (lax.axis_size(axis),) + tile.shape)
    return exchange(spread, axis)


def start_total(tiles):
    return exchange(tiles, "lat")


def total_over_mesh(own):
    own = sum_tiles(gather_tiles(sum_tiles(own), "lon"))
    return gather_tiles(own, "lat")


def moved(block, lat_step, lon_step):
    lats, lons = lax.axis_size("lat"), lax.axis_size("lon")
    if lat_step == 0:
        return lax.ppermute(block, "lon", [(i, (i + lon_step) % lons) for i in range(lons)])
    if lon_step == 0:
        return lax.ppermute(block, "lat", [(i, (i + lat_step) % lats) for i in range(lats)])
    route = [
        (i * lons + j, (i + lat_step) % lats * lons + (j + lon_step) % lons)
        for i in range(lats)
        for j in range(lons)
    ]
    return lax.ppermute(block, ("lat", "lon"), route)


def attended(count, last):
    outs = {
        "xw": ((SLOT * count, D), BF16),
        "cw": ((SLOT * count, D), BF16),
        "blended": ((SLOT * count, D), BF16),
        "back": ((SLOT * count, 3 * D), BF16),
    }
    outs.update(last)
    scratch = [
        pltpu.VMEM((SLOT * count, D), BF16),
        pltpu.VMEM((SLOT * count, 3 * D), BF16),
        pltpu.VMEM((SLOT * count, D), BF16),
        pltpu.VMEM((GROUP, 16, 256), BF16),
    ]
    return outs, scratch


def shards(
    fine_tokens, cotangent, norm_gain, qkv_weight, qkv_down, qkv_up, out_weight, out_down, out_up
):
    lats, lons = lax.axis_size("lat"), lax.axis_size("lon")
    tokens = fine_tokens.reshape(OWN, D)
    cots = cotangent.reshape(OWN, D)
    factors = [x.astype(F32) for x in (qkv_down.T, qkv_up, out_down.T, out_up)]
    pack = jnp.concatenate((*factors, jnp.broadcast_to(norm_gain, (RANK, D))), axis=1)
    weights = {
        "pack": pack,
        "qkv": qkv_weight,
        "out": out_weight,
    }
    pole = (lax.axis_index("lat") == lats - 1).astype(jnp.int32).reshape(1)
    row, col, cor = call(
        send_body,
        {"x": tokens, "c": cots},
        {
            "row": ((2 * ROW_IN, D), BF16),
            "col": ((2 * COL_IN, D), BF16),
            "cor": ((2 * COR_IN, D), BF16),
        },
        "send",
        near=("row", "col", "cor"),
        flops=10**8,
    )
    col = moved(col, 0, -1)
    row = moved(row, -1, 0)
    cor = moved(cor, -1, -1)
    outs, scratch = attended(len(EARLY), {"grads": ((RANK, WIDTH), F32)})
    xw1, cw1, blended1, back1, grads, kept_pack, kept_qkv, kept_out = call(
        early_body,
        {"x": tokens, "c": cots, **weights},
        outs,
        "early",
        scratch=scratch,
        keep=("pack", "qkv", "out"),
        first=("x", "pack"),
        flops=4 * 10**9,
    )
    outs, scratch = attended(len(LATE), {"tiles": ((16, 16, 128), BF16)})
    xw2, cw2, blended2, back2, tiles = call(
        late_body,
        {
            "pole": pole,
            "x": tokens,
            "c": cots,
            "grads": grads,
            "row_in": row,
            "col_in": col,
            "cor_in": cor,
            "pack": kept_pack,
            "qkv": kept_qkv,
            "out": kept_out,
        },
        outs,
        "late",
        scratch=scratch,
        scalars=1,
        near=("row_in", "col_in", "cor_in", "tiles", "pack", "qkv", "out"),
        first=("x", "grads"),
        flops=8 * 10**9,
    )
    own = start_total(tiles)
    mixed, grad, row, col, cor = call(
        finish_body,
        {
            "xw1": xw1,
            "blended1": blended1,
            "pack": pack,
            "out": out_weight,
            "back1": back1,
            "qkv": qkv_weight,
            "cw1": cw1,
            "xw2": xw2,
            "blended2": blended2,
            "back2": back2,
            "cw2": cw2,
        },
        {
            "mixed": ((TOKENS, D), BF16),
            "grad": ((TOKENS, D), BF16),
            "row": ((2 * ROW_OUT, D), BF16),
            "col": ((2 * COL_OUT, D), BF16),
            "cor": ((2 * COR_OUT, D), BF16),
        },
        "finish",
        first=("xw1", "blended1", "pack", "out"),
        near=("row", "col", "cor"),
        flops=3 * 10**9,
    )
    own, mixed, grad, row, col, cor = lax.optimization_barrier((own, mixed, grad, row, col, cor))
    col = moved(col, 0, 1)
    row = moved(row, 1, 0)
    cor = moved(cor, 1, 1)
    tiles = total_over_mesh(own)
    mixed, grad = call(
        place_body,
        {"mixed": mixed, "row": row, "cor": cor, "col": col, "grad": grad},
        {"all_mixed": ((OWN, D), BF16), "all_grad": ((OWN, D), BF16)},
        "place",
        near=("row", "col", "cor"),
        flops=10**9,
    )
    scale = 1.0 / math.sqrt(OWN * lats * lons)

    def last_grads(*refs):
        grads_body(scale, *refs)

    grads = call(
        last_grads,
        {"tiles": tiles},
        dict(zip(GRADS, (((RANK, width), F32) for width in (D, 3 * D, D, D)))),
        "grads",
    )
    shape = (LAT_CELLS, LON_CELLS, D)
    return (
        mixed.reshape(shape),
        grad.reshape(shape),
        grads[0].T,
        grads[1],
        grads[2].T,
        grads[3],
    )


def solution(mesh):
    in_specs = (P("lat", "lon", None), P("lat", "lon", None), P(), P(), P(), P(), P(), P(), P())
    out_specs = (P("lat", "lon", None), P("lat", "lon", None), P(), P(), P(), P())
    return jax.shard_map(shards, mesh=mesh, in_specs=in_specs, out_specs=out_specs, check_vma=False)
```

```python
import math

import jax
import jax.numpy as jnp
from jax import lax
from jax.experimental import pallas as pl
from jax.experimental.pallas import tpu as pltpu
from jax.sharding import PartitionSpec as P

HEADS = 16
WIN_LAT = 6
WIN_LON = 12
HALF_LAT = WIN_LAT // 2
HALF_LON = WIN_LON // 2
LAT_CELLS = 18
LON_CELLS = 24
D = 512
RANK = 8
CELLS = WIN_LAT * WIN_LON
SLOT = 80
BANDS = LAT_CELLS // WIN_LAT
ACROSS = LON_CELLS // WIN_LON
WINDOWS = BANDS * ACROSS
EARLY = ((0, 0), (1, 0))
LATE = ((0, 1), (1, 1), (2, 0), (2, 1))
ORDER = EARLY + LATE
SPAN = 160
TOKENS = WINDOWS * SLOT
OWN = LAT_CELLS * LON_CELLS
HEAD_WIDTH = D // HEADS
GROUP = 256 // HEAD_WIDTH
GROUPS = HEADS // GROUP
STACK = GROUP * SLOT
ROW_IN, COL_IN, COR_IN = 80, 112, 32
COL_FROM, COL_PART = (16, 48, 64), 48
PACK = 2 * RANK
WIDTH = 6 * D
ROW_OUT, COL_OUT, COR_OUT = 64, 96, 32
BF16 = jnp.bfloat16
F32 = jnp.float32
VMEM_ASKED = {"send": 60, "early": 60, "late": 52, "place": 52, "grads": 52}
GRADS = ("qkv_down", "qkv_up", "out_down", "out_up")
FIXED = ("x", "c", "gain", "qkv", "out")


def own_from(a):
    return 64 + 144 * a


def marks_at(shape, source):
    row = lax.broadcasted_iota(jnp.int32, shape, 0)
    lane = lax.broadcasted_iota(jnp.int32, shape, 1)
    return jnp.where(lane == source(row), 1.0, 0.0).astype(BF16)


def over(value, divisor):
    factor, shift = {6: (10923, 16), 12: (10923, 17), 18: (7282, 17), 24: (10923, 18)}[divisor]
    return jnp.right_shift(value * factor, shift)


def pick(test, one, other):
    return jnp.where(test, one, other)


def place_send():
    def source(row):
        at = pick(row < COL_IN, row, row - COL_IN)
        r = over(at, HALF_LON)
        ends = pick(row < COL_IN, HALF_LON * LAT_CELLS, HALF_LON * HALF_LAT)
        return pick(at < ends, LON_CELLS * r + at - HALF_LON * r, -1)

    return marks_at((COL_IN + COR_IN, OWN), source)


def place_in(window, width):
    a, b = window

    def source(cell):
        r = over(cell, WIN_LON)
        c = cell - WIN_LON * r
        row, col = WIN_LAT * a + r + HALF_LAT, WIN_LON * b + c + HALF_LON
        at = LON_CELLS * row + col - own_from(a)
        if b == ACROSS - 1:
            side = SPAN + HALF_LON * row + col - LON_CELLS - COL_FROM[a]
            corner = SPAN + COL_PART + HALF_LON * (row - LAT_CELLS) + col - LON_CELLS
            at = pick(col < LON_CELLS, at, pick(row < LAT_CELLS, side, corner))
        return pick(cell < CELLS, at, -1)

    return marks_at((SLOT, width), source)


def place_last():
    def source(row):
        rho = over(row, LON_CELLS - HALF_LON)
        j = row - (LON_CELLS - HALF_LON) * rho
        cell = WIN_LON * (HALF_LAT + rho) + j
        along = pick(j < WIN_LON, cell, cell + SLOT - WIN_LON)
        along = pick(row < (LON_CELLS - HALF_LON) * HALF_LAT, along, -1)
        at = row - ROW_OUT
        rho = over(jnp.maximum(at, 0), HALF_LON)
        corner = SLOT + WIN_LON * (HALF_LAT + rho) + HALF_LON + at - HALF_LON * rho
        corner = pick(at < HALF_LON * HALF_LAT, corner, -1)
        return pick(row < ROW_OUT, along, corner)

    return marks_at((ROW_OUT + COR_OUT, ACROSS * SLOT), source)


def place_side():
    def source(row):
        i = over(row, HALF_LON)
        a = over(i, WIN_LAT)
        cell = WIN_LON * (i - WIN_LAT * a) + HALF_LON + row - HALF_LON * i
        return pick(row < HALF_LON * (LAT_CELLS - HALF_LAT), SLOT * a + cell, -1)

    return marks_at((COL_OUT, BANDS * SLOT), source)


def place_out(at):
    def source(row):
        r = over(row, LON_CELLS)
        col = row - LON_CELLS * r
        i, j = WIN_LAT * at + r - HALF_LAT, col - HALF_LON
        late = r >= HALF_LAT
        cell = WIN_LON * pick(late, r - HALF_LAT, r + HALF_LAT) + j
        cell = pick(j < WIN_LON, cell, cell + SLOT - WIN_LON)
        inner = pick(late, SPAN + cell, cell)
        edge = 2 * SPAN + HALF_LON * i + col
        if at == 0:
            inner = pick(late, inner, (LON_CELLS - HALF_LON) * r + j)
            edge = pick(late, edge, ROW_OUT + HALF_LON * r + col)
        return pick(j < 0, edge, inner)

    return marks_at((WIN_LAT * LON_CELLS, 2 * SPAN + COL_OUT), source)


def head_marks():
    lane = lax.broadcasted_iota(jnp.int32, (16, 256), 1)
    heads = [
        jnp.where(jnp.right_shift(lane, 5) == head, 1.0, 0.0).astype(BF16)
        for head in range(GROUP)
    ]
    return jnp.stack(heads, axis=0)


def nn(left, right):
    return lax.dot_general(left, right, (((1,), (0,)), ((), ())), preferred_element_type=F32)


def nt(left, right):
    return lax.dot_general(left, right, (((1,), (1,)), ((), ())), preferred_element_type=F32)


class Staged:
    def __init__(self, names, outside, buffers, sem):
        self.copies = {x: (outside[x], buffers[x], sem[x]) for x in names if x in buffers}
        self.buffers = {x: buffers.get(x, outside[x]) for x in names}
        self.open = {}

    def fetch(self):
        for name, (ref, buffer, sem) in self.copies.items():
            self.open[name] = pltpu.make_async_copy(ref, buffer, sem)
            self.open[name].start()

    def __getitem__(self, name):
        if name in self.open:
            self.open.pop(name).wait()
        return self.buffers[name]

    def send(self, *names):
        for name in names:
            if name not in self.copies:
                continue
            ref, buffer, sem = self.copies[name]
            self.open[name] = pltpu.make_async_copy(buffer, ref, sem)
            self.open[name].start()

    def close(self):
        for name in list(self.open):
            self.open.pop(name).wait()


def call(body, ins, outs, name, scratch=(), scalars=0, near=(), keep=(), flops=0):
    arrays = list(ins.values())
    outs = dict(outs, **{x + "_kept": (ins[x].shape, ins[x].dtype) for x in keep})
    in_names, out_names = list(ins)[scalars:], list(outs)
    near = (*near, *(x + "_kept" for x in keep))
    shapes = [jax.ShapeDtypeStruct(shape, dtype) for shape, dtype in outs.values()]
    names = in_names + out_names
    far = [x for x in names if x not in near]
    own = [x for x in far if x not in keep]
    kinds = dict(zip(names, arrays[scalars:] + shapes))

    def kernel(*refs):
        heads, refs = refs[:scalars], refs[scalars:]
        outside, refs = dict(zip(names, refs)), refs[len(names) :]
        buffers, refs = dict(zip(own, refs)), refs[len(own) :]
        buffers.update({x: outside[x + "_kept"] for x in keep})
        sems, rest = refs[0], refs[1:]
        sem = {x: sems.at[at] for at, x in enumerate(far)}
        given = Staged(in_names, outside, buffers, sem)
        made = Staged(out_names, outside, buffers, sem)
        given.fetch()
        body(given, made, *heads, *rest)
        given.close()
        made.close()

    def spec(x):
        if x in near:
            return pl.BlockSpec(memory_space=pltpu.VMEM)
        return pl.BlockSpec(memory_space=pltpu.HBM if x in FIXED else pl.ANY)

    return pl.pallas_call(
        kernel,
        out_shape=shapes,
        in_specs=[pl.BlockSpec(memory_space=pltpu.SMEM)] * scalars + [spec(x) for x in in_names],
        out_specs=[spec(x) for x in out_names],
        scratch_shapes=[pltpu.VMEM(kinds[x].shape, kinds[x].dtype) for x in own]
        + [pltpu.SemaphoreType.DMA((max(len(far), 1),))]
        + list(scratch),
        compiler_params=pltpu.CompilerParams(vmem_limit_bytes=VMEM_ASKED[name] << 20),
        cost_estimate=pl.CostEstimate(
            flops=flops, bytes_accessed=4 * 1024 * 1024, transcendentals=0
        ),
        name=name,
    )(*arrays)


def send_body(given, made):
    place = place_send()
    for at, name in enumerate(("x", "c")):
        ref = given[name]
        made["row"][ROW_IN * at : ROW_IN * (at + 1)] = ref[:ROW_IN]
        picked = nn(place, ref[...]).astype(BF16)
        made["col"][COL_IN * at : COL_IN * (at + 1)] = picked[:COL_IN]
        made["cor"][COR_IN * at : COR_IN * (at + 1)] = picked[COL_IN:]
    made.send("col", "row", "cor")


def split_heads(block, marks):
    tiles = block.reshape(1, SLOT // 16, 16, 256) * marks[:, None]
    return tiles.reshape(STACK, 256)


def join_heads(stacked):
    lane = lax.broadcasted_iota(jnp.int32, (SLOT, 128), 1)
    parts = [stacked[SLOT * h : SLOT * (h + 1)] for h in range(4)]
    low = jnp.where(lane < 32, parts[0], parts[1])
    high = jnp.where(lane < 96, parts[2], parts[3])
    return jnp.where(lane < 64, low, high)


def per_query(weights, block):
    turned = weights.T
    half = STACK // 2
    return jnp.concatenate(
        (
            join_heads(nn(turned[:half], block[:, :128])),
            join_heads(nn(turned[half:], block[:, 128:])),
        ),
        axis=1,
    )


def adapters(pack_ref):
    return (
        pack_ref[:, :D],
        pack_ref[:, D : 4 * D],
        pack_ref[:, 4 * D : 5 * D],
        pack_ref[:, 5 * D :],
    )


def attend(given, made, windows, blocks, ended, pole, tokens, cots, hidden, packed, bblend, blended_ref, back_ref, marks_ref, apart_ref):
    count = len(windows)
    for first in range(0, count, 2):
        rows = pl.ds(SLOT * first, 2 * SLOT)
        blocks(given, tokens, cots, first)
        wide = tokens[rows].astype(F32)
        center = wide - jnp.mean(wide, axis=-1, keepdims=True)
        spread = jnp.mean(center * center, axis=-1, keepdims=True)
        normed = (center * lax.rsqrt(spread + 1e-05) * given["gain"][...]).astype(BF16)
        hidden[rows] = normed
        down, up, odown, oup = adapters(given["pack"])
        low = nt(normed, down).astype(BF16)
        packed[rows] = (nn(normed, given["qkv"][...]) + nn(low, up)).astype(BF16)
        cot = cots[rows]
        back_low = nt(cot, oup).astype(BF16)
        bblend[rows] = (nt(cot, given["out"][...]) + nn(back_low, odown)).astype(BF16)

    marks_ref[...] = head_marks()
    rest = jnp.zeros((SLOT - CELLS, STACK), F32)
    scale = 1.0 / math.sqrt(HEAD_WIDTH)
    marks = marks_ref[...]
    if pole is not None:
        key_late = lax.broadcasted_iota(jnp.int32, (CELLS, STACK), 0) >= CELLS // 2
        query_at = lax.rem(lax.broadcasted_iota(jnp.int32, (CELLS, STACK), 1), SLOT)
        cut = jnp.where(pole > 0, -1e30, 0.0)
        apart_ref[...] = (key_late != (query_at >= CELLS // 2)).astype(F32) * cut

    for w, (a, _) in enumerate(windows):
        rows = pl.ds(w * SLOT, SLOT)
        for g in range(GROUPS):
            at = 256 * g
            query = packed[rows, at : at + 256]
            key = packed[rows, D + at : D + at + 256]
            value = packed[rows, 2 * D + at : 2 * D + at + 256]
            back = bblend[rows, at : at + 256]
            queries = split_heads(query, marks)
            backs = split_heads(back, marks)
            scores = nt(key, queries)[:CELLS]
            if a == BANDS - 1:
                scores = scores + apart_ref[...]
            top = jnp.max(scores, axis=0, keepdims=True)
            exponent = jnp.exp2((scores - top) * (scale * math.log2(math.e)))
            weights = exponent * (1.0 / jnp.sum(exponent, axis=0, keepdims=True))
            rounded = jnp.concatenate((weights, rest), axis=0).astype(BF16)
            blended_ref[rows, at : at + 256] = per_query(rounded, value).astype(BF16)
            back_weights = nt(value, backs)[:CELLS].astype(BF16).astype(F32)
            total = jnp.sum(weights * back_weights, axis=0, keepdims=True)
            back_scores = (weights * scale) * (back_weights - total)
            back_scores = jnp.concatenate((back_scores, rest), axis=0).astype(BF16)
            back_ref[rows, at : at + 256] = per_query(back_scores, key).astype(BF16)
            back_ref[rows, D + at : D + at + 256] = nn(back_scores, queries).astype(BF16)
            back_ref[rows, 2 * D + at : 2 * D + at + 256] = nn(rounded, backs).astype(BF16)

    for first in range(0, count, 2):
        rows = pl.ds(SLOT * first, 2 * SLOT)
        wide = tokens[rows].astype(F32)
        blended = blended_ref[rows]
        low = nt(blended, odown).astype(BF16)
        update = (nn(blended, given["out"][...]) + nn(low, oup)).astype(BF16)
        made["mixed"][rows] = (wide + update.astype(F32)).astype(BF16)
        back = back_ref[rows]
        back_low = nt(back, up).astype(BF16)
        back_hidden = nt(back, given["qkv"][...]) + nn(back_low, down)
        center = wide - jnp.mean(wide, axis=-1, keepdims=True)
        spread = jnp.mean(center * center, axis=-1, keepdims=True)
        inverse = lax.rsqrt(spread + 1e-05)
        normed = center * inverse
        scaled = back_hidden * given["gain"][...]
        along = jnp.mean(scaled * normed, axis=-1, keepdims=True)
        across = jnp.mean(scaled, axis=-1, keepdims=True)
        change = (inverse * (scaled - across - normed * along)).astype(BF16).astype(F32)
        made["grad"][rows] = (cots[rows].astype(F32) + change).astype(BF16)
    made.send("mixed", "grad")
    ended(made)
    cot = cots[...]
    blended = blended_ref[...]
    back = back_ref[...]
    return jnp.concatenate(
        (
            nn(nt(up, back).astype(BF16), hidden[...])[:RANK],
            nn(nt(down, hidden[...]).astype(BF16), back)[:RANK],
            nn(nt(oup, cot).astype(BF16), blended)[:RANK],
            nn(nt(odown, blended).astype(BF16), cot)[:RANK],
        ),
        axis=1,
    )


def early_blocks(given, tokens, cots, first):
    for k in range(first, first + 2):
        begin = own_from(EARLY[k][0])
        place = place_in(EARLY[k], SPAN)
        for source, into in (("x", tokens), ("c", cots)):
            own = given[source][begin : begin + SPAN]
            into[SLOT * k : SLOT * (k + 1)] = nn(place, own).astype(BF16)


def late_blocks(given, tokens, cots, first):
    for k in range(first, first + 2):
        a, b = LATE[k]
        begin = own_from(a)
        place = place_in(LATE[k], SPAN + COL_PART + COR_IN)
        for at, (source, into) in enumerate((("x", tokens), ("c", cots))):
            if a < BANDS - 1:
                own = given[source][begin : begin + SPAN]
            else:
                row = given["row_in"][ROW_IN * at : ROW_IN * (at + 1)]
                own = jnp.concatenate((given[source][begin:], row), axis=0)
            side = given["col_in"][pl.ds(COL_IN * at + COL_FROM[a], COL_PART)]
            corner = given["cor_in"][COR_IN * at : COR_IN * (at + 1)]
            block = jnp.concatenate((own, side, corner), axis=0)
            into[SLOT * k : SLOT * (k + 1)] = nn(place, block).astype(BF16)


def early_ended(made):
    pass


def late_ended(made):
    last, side = place_last(), place_side()
    for at, name in enumerate(("mixed", "grad")):
        ref = made.buffers[name]
        ends = nn(last, ref[SLOT * (len(LATE) - 2) :]).astype(BF16)
        made["row"][ROW_OUT * at : ROW_OUT * (at + 1)] = ends[:ROW_OUT]
        made["cor"][COR_OUT * at : COR_OUT * (at + 1)] = ends[ROW_OUT:]
        beyond = [ref[SLOT * k : SLOT * (k + 1)] for k in (0, 1, 3)]
        picked = nn(side, jnp.concatenate(beyond, axis=0)).astype(BF16)
        made["col"][COL_OUT * at : COL_OUT * (at + 1)] = picked
    made.send("col", "row", "cor")


def early_body(given, made, *scratch):
    grads = attend(given, made, EARLY, early_blocks, early_ended, None, *scratch)
    made["grads"][...] = grads
    made.send("grads")


def late_body(given, made, pole_ref, *scratch):
    grads = attend(given, made, LATE, late_blocks, late_ended, pole_ref[0], *scratch)
    grads = grads + given["grads"][...]
    tiles = made["tiles"]
    for owner in range(16):
        at = 256 * owner
        if at < WIDTH:
            both = (grads[:, at : at + 128], grads[:, at + 128 : at + 256])
            tiles[owner] = jnp.concatenate(both, axis=0).astype(BF16)
        else:
            tiles[owner] = jnp.zeros((16, 128), BF16)
    made.send("tiles")


def place_body(given, made):
    rows = WIN_LAT * LON_CELLS
    places = [place_out(a) for a in range(BANDS)]
    for at, name in enumerate(("mixed", "grad")):
        parts = {EARLY: given[name + "1"], LATE: given[name + "2"]}

        def window(where):
            part = EARLY if where in EARLY else LATE
            k = part.index(where)
            return parts[part][SLOT * k : SLOT * (k + 1)]

        def band(a):
            return [window((a, b)) for b in range(ACROSS)]

        for a in range(BANDS):
            if a:
                before = band(a - 1)
            else:
                before = [
                    given["row"][ROW_OUT * at : ROW_OUT * (at + 1)],
                    given["cor"][COR_OUT * at : COR_OUT * (at + 1)],
                    window((0, 0))[: SPAN - ROW_OUT - COR_OUT],
                ]
            side = given["col"][COL_OUT * at : COL_OUT * (at + 1)]
            source = jnp.concatenate((*before, *band(a), side), axis=0)
            out = made["all_" + name]
            out[rows * a : rows * (a + 1)] = nn(places[a], source).astype(BF16)
        made.send("all_" + name)


def grads_body(scale, given, made):
    tile = 0
    for name in GRADS:
        ref = made[name]
        for at in range(ref.shape[1] // 128):
            owner, row = tile // 2, RANK * (tile % 2)
            wide = given["tiles"][owner].astype(F32) * scale
            ref[:, 128 * at : 128 * (at + 1)] = wide[row : row + RANK]
            tile += 1
    made.send(*GRADS)


def exchange(tiles, axis):
    return lax.all_to_all(tiles, axis, 0, 0, tiled=True)


def sum_tiles(tiles):
    return jnp.sum(tiles.astype(F32), axis=0).astype(BF16)


def gather_tiles(tile, axis):
    spread = jnp.broadcast_to(tile[None], (lax.axis_size(axis),) + tile.shape)
    return exchange(spread, axis)


def start_total(tiles):
    return exchange(tiles, "lat")


def total_over_mesh(own):
    own = sum_tiles(gather_tiles(sum_tiles(own), "lon"))
    return gather_tiles(own, "lat")


def moved(block, lat_step, lon_step):
    lats, lons = lax.axis_size("lat"), lax.axis_size("lon")
    if lat_step == 0:
        return lax.ppermute(block, "lon", [(i, (i + lon_step) % lons) for i in range(lons)])
    if lon_step == 0:
        return lax.ppermute(block, "lat", [(i, (i + lat_step) % lats) for i in range(lats)])
    route = [
        (i * lons + j, (i + lat_step) % lats * lons + (j + lon_step) % lons)
        for i in range(lats)
        for j in range(lons)
    ]
    return lax.ppermute(block, ("lat", "lon"), route)


def attended(count, last):
    outs = {"mixed": ((SLOT * count, D), BF16), "grad": ((SLOT * count, D), BF16)}
    outs.update(last)
    widths = (D, D, D, 3 * D, D, D, 3 * D)
    scratch = [pltpu.VMEM((SLOT * count, width), BF16) for width in widths]
    return outs, scratch + [pltpu.VMEM((GROUP, 16, 256), BF16), pltpu.VMEM((CELLS, STACK), F32)]


def shards(
    fine_tokens, cotangent, norm_gain, qkv_weight, qkv_down, qkv_up, out_weight, out_down, out_up
):
    lats, lons = lax.axis_size("lat"), lax.axis_size("lon")
    tokens = fine_tokens.reshape(OWN, D)
    cots = cotangent.reshape(OWN, D)
    pack = jnp.concatenate((qkv_down.T, qkv_up, out_down.T, out_up), axis=1)
    pack = jnp.pad(pack, ((0, PACK - RANK), (0, 0)))
    weights = {
        "gain": norm_gain.reshape(1, D),
        "pack": pack,
        "qkv": qkv_weight,
        "out": out_weight,
    }
    pole = (lax.axis_index("lat") == lats - 1).astype(jnp.int32).reshape(1)
    row, col, cor = call(
        send_body,
        {"x": tokens, "c": cots},
        {
            "row": ((2 * ROW_IN, D), BF16),
            "col": ((2 * COL_IN, D), BF16),
            "cor": ((2 * COR_IN, D), BF16),
        },
        "send",
        near=("row", "col", "cor"),
        flops=10**8,
    )
    col = moved(col, 0, -1)
    row = moved(row, -1, 0)
    cor = moved(cor, -1, -1)
    outs, scratch = attended(len(EARLY), {"grads": ((RANK, WIDTH), F32)})
    mixed1, grad1, grads = call(
        early_body,
        {"x": tokens, "c": cots, **weights},
        outs,
        "early",
        scratch=scratch,
        flops=4 * 10**9,
    )
    last = {
        "tiles": ((16, 16, 128), BF16),
        "row": ((2 * ROW_OUT, D), BF16),
        "col": ((2 * COL_OUT, D), BF16),
        "cor": ((2 * COR_OUT, D), BF16),
    }
    outs, scratch = attended(len(LATE), last)
    mixed2, grad2, tiles, row, col, cor = call(
        late_body,
        {
            "pole": pole,
            "x": tokens,
            "c": cots,
            **weights,
            "grads": grads,
            "row_in": row,
            "col_in": col,
            "cor_in": cor,
        },
        outs,
        "late",
        scratch=scratch,
        scalars=1,
        near=("row_in", "col_in", "cor_in"),
        flops=8 * 10**9,
    )
    own = start_total(tiles)
    col = moved(col, 0, 1)
    own, row, cor = lax.optimization_barrier((own, row, cor))
    row = moved(row, 1, 0)
    cor = moved(cor, 1, 1)
    tiles = total_over_mesh(own)
    mixed, grad = call(
        place_body,
        {
            "mixed1": mixed1,
            "mixed2": mixed2,
            "row": row,
            "cor": cor,
            "col": col,
            "grad1": grad1,
            "grad2": grad2,
        },
        {"all_mixed": ((OWN, D), BF16), "all_grad": ((OWN, D), BF16)},
        "place",
        near=("row", "col", "cor"),
        flops=10**9,
    )
    scale = 1.0 / math.sqrt(OWN * lats * lons)

    def last_grads(*refs):
        grads_body(scale, *refs)

    grads = call(
        last_grads,
        {"tiles": tiles},
        dict(zip(GRADS, (((RANK, width), F32) for width in (D, 3 * D, D, D)))),
        "grads",
    )
    shape = (LAT_CELLS, LON_CELLS, D)
    return (
        mixed.reshape(shape),
        grad.reshape(shape),
        grads[0].T,
        grads[1],
        grads[2].T,
        grads[3],
    )


def solution(mesh):
    in_specs = (P("lat", "lon", None), P("lat", "lon", None), P(), P(), P(), P(), P(), P(), P())
    out_specs = (P("lat", "lon", None), P("lat", "lon", None), P(), P(), P(), P())
    return jax.shard_map(shards, mesh=mesh, in_specs=in_specs, out_specs=out_specs, check_vma=False)
```

```python
import math

import jax
import jax.numpy as jnp
from jax import lax
from jax.experimental import pallas as pl
from jax.experimental.pallas import tpu as pltpu
from jax.sharding import PartitionSpec as P

HEADS = 16
WIN_LAT = 6
WIN_LON = 12
HALF_LAT = WIN_LAT // 2
HALF_LON = WIN_LON // 2
LAT_CELLS = 18
LON_CELLS = 24
D = 512
RANK = 8
CELLS = WIN_LAT * WIN_LON
SLOT = 80
BANDS = LAT_CELLS // WIN_LAT
ACROSS = LON_CELLS // WIN_LON
WINDOWS = BANDS * ACROSS
EARLY = ((0, 0), (1, 0))
LATE = ((0, 1), (1, 1), (2, 0), (2, 1))
ORDER = EARLY + LATE
SPAN = 160
TOKENS = WINDOWS * SLOT
OWN = LAT_CELLS * LON_CELLS
HEAD_WIDTH = D // HEADS
GROUP = 256 // HEAD_WIDTH
GROUPS = HEADS // GROUP
STACK = GROUP * SLOT
ROW_IN, COL_IN, COR_IN = 80, 112, 32
COL_FROM, COL_PART = (16, 48, 64), 48
PACK = 2 * RANK
WIDTH = 6 * D
ROW_OUT, COL_OUT, COR_OUT = 64, 96, 32
BF16 = jnp.bfloat16
F32 = jnp.float32
VMEM_ASKED = {"send": 60, "early": 60, "late": 52, "finish": 50, "place": 52, "grads": 52}
GRADS = ("qkv_down", "qkv_up", "out_down", "out_up")
FIXED = ("x", "c", "gain", "qkv", "out")


def own_from(a):
    return 64 + 144 * a


def marks_at(shape, source):
    row = lax.broadcasted_iota(jnp.int32, shape, 0)
    lane = lax.broadcasted_iota(jnp.int32, shape, 1)
    return jnp.where(lane == source(row), 1.0, 0.0).astype(BF16)


def over(value, divisor):
    factor, shift = {6: (10923, 16), 12: (10923, 17), 18: (7282, 17), 24: (10923, 18)}[divisor]
    return jnp.right_shift(value * factor, shift)


def pick(test, one, other):
    return jnp.where(test, one, other)


def place_send():
    def source(row):
        at = pick(row < COL_IN, row, row - COL_IN)
        r = over(at, HALF_LON)
        ends = pick(row < COL_IN, HALF_LON * LAT_CELLS, HALF_LON * HALF_LAT)
        return pick(at < ends, LON_CELLS * r + at - HALF_LON * r, -1)

    return marks_at((COL_IN + COR_IN, OWN), source)


def place_in(window, width):
    a, b = window

    def source(cell):
        r = over(cell, WIN_LON)
        c = cell - WIN_LON * r
        row, col = WIN_LAT * a + r + HALF_LAT, WIN_LON * b + c + HALF_LON
        at = LON_CELLS * row + col - own_from(a)
        if b == ACROSS - 1:
            side = SPAN + HALF_LON * row + col - LON_CELLS - COL_FROM[a]
            corner = SPAN + COL_PART + HALF_LON * (row - LAT_CELLS) + col - LON_CELLS
            at = pick(col < LON_CELLS, at, pick(row < LAT_CELLS, side, corner))
        return pick(cell < CELLS, at, -1)

    return marks_at((SLOT, width), source)


def place_last():
    def source(row):
        rho = over(row, LON_CELLS - HALF_LON)
        j = row - (LON_CELLS - HALF_LON) * rho
        cell = WIN_LON * (HALF_LAT + rho) + j
        along = pick(j < WIN_LON, cell, cell + SLOT - WIN_LON)
        along = pick(row < (LON_CELLS - HALF_LON) * HALF_LAT, along, -1)
        at = row - ROW_OUT
        rho = over(jnp.maximum(at, 0), HALF_LON)
        corner = SLOT + WIN_LON * (HALF_LAT + rho) + HALF_LON + at - HALF_LON * rho
        corner = pick(at < HALF_LON * HALF_LAT, corner, -1)
        return pick(row < ROW_OUT, along, corner)

    return marks_at((ROW_OUT + COR_OUT, ACROSS * SLOT), source)


def place_side():
    def source(row):
        i = over(row, HALF_LON)
        a = over(i, WIN_LAT)
        cell = WIN_LON * (i - WIN_LAT * a) + HALF_LON + row - HALF_LON * i
        return pick(row < HALF_LON * (LAT_CELLS - HALF_LAT), SLOT * a + cell, -1)

    return marks_at((COL_OUT, BANDS * SLOT), source)


def place_out(at):
    def source(row):
        r = over(row, LON_CELLS)
        col = row - LON_CELLS * r
        i, j = WIN_LAT * at + r - HALF_LAT, col - HALF_LON
        late = r >= HALF_LAT
        cell = WIN_LON * pick(late, r - HALF_LAT, r + HALF_LAT) + j
        cell = pick(j < WIN_LON, cell, cell + SLOT - WIN_LON)
        inner = pick(late, SPAN + cell, cell)
        edge = 2 * SPAN + HALF_LON * i + col
        if at == 0:
            inner = pick(late, inner, (LON_CELLS - HALF_LON) * r + j)
            edge = pick(late, edge, ROW_OUT + HALF_LON * r + col)
        return pick(j < 0, edge, inner)

    return marks_at((WIN_LAT * LON_CELLS, 2 * SPAN + COL_OUT), source)


def head_marks():
    lane = lax.broadcasted_iota(jnp.int32, (16, 256), 1)
    heads = [
        jnp.where(jnp.right_shift(lane, 5) == head, 1.0, 0.0).astype(BF16)
        for head in range(GROUP)
    ]
    return jnp.stack(heads, axis=0)


def nn(left, right):
    return lax.dot_general(left, right, (((1,), (0,)), ((), ())), preferred_element_type=F32)


def nt(left, right):
    return lax.dot_general(left, right, (((1,), (1,)), ((), ())), preferred_element_type=F32)


class Staged:
    def __init__(self, names, outside, buffers, sem):
        self.copies = {x: (outside[x], buffers[x], sem[x]) for x in names if x in buffers}
        self.buffers = {x: buffers.get(x, outside[x]) for x in names}
        self.open = {}

    def fetch(self):
        for name, (ref, buffer, sem) in self.copies.items():
            self.open[name] = pltpu.make_async_copy(ref, buffer, sem)
            self.open[name].start()

    def __getitem__(self, name):
        if name in self.open:
            self.open.pop(name).wait()
        return self.buffers[name]

    def send(self, *names):
        for name in names:
            if name not in self.copies:
                continue
            ref, buffer, sem = self.copies[name]
            self.open[name] = pltpu.make_async_copy(buffer, ref, sem)
            self.open[name].start()

    def close(self):
        for name in list(self.open):
            self.open.pop(name).wait()


def call(body, ins, outs, name, scratch=(), scalars=0, near=(), keep=(), flops=0):
    arrays = list(ins.values())
    outs = dict(outs, **{x + "_kept": (ins[x].shape, ins[x].dtype) for x in keep})
    in_names, out_names = list(ins)[scalars:], list(outs)
    near = (*near, *(x + "_kept" for x in keep))
    shapes = [jax.ShapeDtypeStruct(shape, dtype) for shape, dtype in outs.values()]
    names = in_names + out_names
    far = [x for x in names if x not in near]
    own = [x for x in far if x not in keep]
    kinds = dict(zip(names, arrays[scalars:] + shapes))

    def kernel(*refs):
        heads, refs = refs[:scalars], refs[scalars:]
        outside, refs = dict(zip(names, refs)), refs[len(names) :]
        buffers, refs = dict(zip(own, refs)), refs[len(own) :]
        buffers.update({x: outside[x + "_kept"] for x in keep})
        sems, rest = refs[0], refs[1:]
        sem = {x: sems.at[at] for at, x in enumerate(far)}
        given = Staged(in_names, outside, buffers, sem)
        made = Staged(out_names, outside, buffers, sem)
        given.fetch()
        body(given, made, *heads, *rest)
        given.close()
        made.close()

    def spec(x):
        if x in near:
            return pl.BlockSpec(memory_space=pltpu.VMEM)
        return pl.BlockSpec(memory_space=pltpu.HBM if x in FIXED else pl.ANY)

    return pl.pallas_call(
        kernel,
        out_shape=shapes,
        in_specs=[pl.BlockSpec(memory_space=pltpu.SMEM)] * scalars + [spec(x) for x in in_names],
        out_specs=[spec(x) for x in out_names],
        scratch_shapes=[pltpu.VMEM(kinds[x].shape, kinds[x].dtype) for x in own]
        + [pltpu.SemaphoreType.DMA((max(len(far), 1),))]
        + list(scratch),
        compiler_params=pltpu.CompilerParams(vmem_limit_bytes=VMEM_ASKED[name] << 20),
        cost_estimate=pl.CostEstimate(
            flops=flops, bytes_accessed=4 * 1024 * 1024, transcendentals=0
        ),
        name=name,
    )(*arrays)


def send_body(given, made):
    place = place_send()
    for at, name in enumerate(("x", "c")):
        ref = given[name]
        made["row"][ROW_IN * at : ROW_IN * (at + 1)] = ref[:ROW_IN]
        picked = nn(place, ref[...]).astype(BF16)
        made["col"][COL_IN * at : COL_IN * (at + 1)] = picked[:COL_IN]
        made["cor"][COR_IN * at : COR_IN * (at + 1)] = picked[COL_IN:]
    made.send("col", "row", "cor")


def split_heads(block, marks):
    tiles = block.reshape(1, SLOT // 16, 16, 256) * marks[:, None]
    return tiles.reshape(STACK, 256)


def join_heads(stacked):
    lane = lax.broadcasted_iota(jnp.int32, (SLOT, 128), 1)
    parts = [stacked[SLOT * h : SLOT * (h + 1)] for h in range(4)]
    low = jnp.where(lane < 32, parts[0], parts[1])
    high = jnp.where(lane < 96, parts[2], parts[3])
    return jnp.where(lane < 64, low, high)


def per_query(weights, block):
    turned = weights.T
    half = STACK // 2
    return jnp.concatenate(
        (
            join_heads(nn(turned[:half], block[:, :128])),
            join_heads(nn(turned[half:], block[:, 128:])),
        ),
        axis=1,
    )


def adapters(pack_ref):
    return (
        pack_ref[:, :D],
        pack_ref[:, D : 4 * D],
        pack_ref[:, 4 * D : 5 * D],
        pack_ref[:, 5 * D :],
    )


def finish(given, made, count, tokens, cots, blended_ref, back_ref):
    down, up, odown, oup = adapters(given["pack"])
    blocks = [pl.ds(SLOT * first, 2 * SLOT) for first in range(0, count, 2)]
    for rows in blocks:
        wide = tokens()[rows].astype(F32)
        blended = blended_ref()[rows]
        low = nt(blended, odown).astype(BF16)
        update = (nn(blended, given["out"][...]) + nn(low, oup)).astype(BF16)
        made["mixed"][rows] = (wide + update.astype(F32)).astype(BF16)
    made.send("mixed")
    for rows in blocks:
        wide = tokens()[rows].astype(F32)
        back = back_ref()[rows]
        back_low = nt(back, up).astype(BF16)
        back_hidden = nt(back, given["qkv"][...]) + nn(back_low, down)
        center = wide - jnp.mean(wide, axis=-1, keepdims=True)
        spread = jnp.mean(center * center, axis=-1, keepdims=True)
        inverse = lax.rsqrt(spread + 1e-05)
        normed = center * inverse
        scaled = back_hidden * given["gain"][...]
        along = jnp.mean(scaled * normed, axis=-1, keepdims=True)
        across = jnp.mean(scaled, axis=-1, keepdims=True)
        change = (inverse * (scaled - across - normed * along)).astype(BF16).astype(F32)
        made["grad"][rows] = (cots()[rows].astype(F32) + change).astype(BF16)
    made.send("grad")


def attend(given, made, windows, blocks, pole, places, hidden, packed, bblend, marks_ref, apart_ref):
    tokens, cots, blended_ref, back_ref = places
    count = len(windows)
    for first in range(0, count, 2):
        rows = pl.ds(SLOT * first, 2 * SLOT)
        blocks(given, tokens, cots, first)
        wide = tokens[rows].astype(F32)
        center = wide - jnp.mean(wide, axis=-1, keepdims=True)
        spread = jnp.mean(center * center, axis=-1, keepdims=True)
        normed = (center * lax.rsqrt(spread + 1e-05) * given["gain"][...]).astype(BF16)
        hidden[rows] = normed
        down, up, odown, oup = adapters(given["pack"])
        low = nt(normed, down).astype(BF16)
        packed[rows] = (nn(normed, given["qkv"][...]) + nn(low, up)).astype(BF16)
        cot = cots[rows]
        back_low = nt(cot, oup).astype(BF16)
        bblend[rows] = (nt(cot, given["out"][...]) + nn(back_low, odown)).astype(BF16)

    marks_ref[...] = head_marks()
    rest = jnp.zeros((SLOT - CELLS, STACK), F32)
    scale = 1.0 / math.sqrt(HEAD_WIDTH)
    marks = marks_ref[...]
    if pole is not None:
        key_late = lax.broadcasted_iota(jnp.int32, (CELLS, STACK), 0) >= CELLS // 2
        query_at = lax.rem(lax.broadcasted_iota(jnp.int32, (CELLS, STACK), 1), SLOT)
        cut = jnp.where(pole > 0, -1e30, 0.0)
        apart_ref[...] = (key_late != (query_at >= CELLS // 2)).astype(F32) * cut

    for w, (a, _) in enumerate(windows):
        rows = pl.ds(w * SLOT, SLOT)
        for g in range(GROUPS):
            at = 256 * g
            query = packed[rows, at : at + 256]
            key = packed[rows, D + at : D + at + 256]
            value = packed[rows, 2 * D + at : 2 * D + at + 256]
            back = bblend[rows, at : at + 256]
            queries = split_heads(query, marks)
            backs = split_heads(back, marks)
            scores = nt(key, queries)[:CELLS]
            if a == BANDS - 1:
                scores = scores + apart_ref[...]
            top = jnp.max(scores, axis=0, keepdims=True)
            exponent = jnp.exp2((scores - top) * (scale * math.log2(math.e)))
            weights = exponent * (1.0 / jnp.sum(exponent, axis=0, keepdims=True))
            rounded = jnp.concatenate((weights, rest), axis=0).astype(BF16)
            blended_ref[rows, at : at + 256] = per_query(rounded, value).astype(BF16)
            back_weights = nt(value, backs)[:CELLS].astype(BF16).astype(F32)
            total = jnp.sum(weights * back_weights, axis=0, keepdims=True)
            back_scores = (weights * scale) * (back_weights - total)
            back_scores = jnp.concatenate((back_scores, rest), axis=0).astype(BF16)
            back_ref[rows, at : at + 256] = per_query(back_scores, key).astype(BF16)
            back_ref[rows, D + at : D + at + 256] = nn(back_scores, queries).astype(BF16)
            back_ref[rows, 2 * D + at : 2 * D + at + 256] = nn(rounded, backs).astype(BF16)

    made.send("xw", "cw", "blended", "back")
    down, up, odown, oup = adapters(given["pack"])
    if "mixed" in made.buffers:
        finish(given, made, count, *(lambda x=x: x for x in places))
    cot = cots[...]
    blended = blended_ref[...]
    back = back_ref[...]
    return jnp.concatenate(
        (
            nn(nt(up, back).astype(BF16), hidden[...])[:RANK],
            nn(nt(down, hidden[...]).astype(BF16), back)[:RANK],
            nn(nt(oup, cot).astype(BF16), blended)[:RANK],
            nn(nt(odown, blended).astype(BF16), cot)[:RANK],
        ),
        axis=1,
    )


def early_blocks(given, tokens, cots, first):
    for k in range(first, first + 2):
        begin = own_from(EARLY[k][0])
        place = place_in(EARLY[k], SPAN)
        for source, into in (("x", tokens), ("c", cots)):
            own = given[source][begin : begin + SPAN]
            into[SLOT * k : SLOT * (k + 1)] = nn(place, own).astype(BF16)


def late_blocks(given, tokens, cots, first):
    for k in range(first, first + 2):
        a, b = LATE[k]
        begin = own_from(a)
        place = place_in(LATE[k], SPAN + COL_PART + COR_IN)
        for at, (source, into) in enumerate((("x", tokens), ("c", cots))):
            if a < BANDS - 1:
                own = given[source][begin : begin + SPAN]
            else:
                row = given["row_in"][ROW_IN * at : ROW_IN * (at + 1)]
                own = jnp.concatenate((given[source][begin:], row), axis=0)
            side = given["col_in"][pl.ds(COL_IN * at + COL_FROM[a], COL_PART)]
            corner = given["cor_in"][COR_IN * at : COR_IN * (at + 1)]
            block = jnp.concatenate((own, side, corner), axis=0)
            into[SLOT * k : SLOT * (k + 1)] = nn(place, block).astype(BF16)


def send_back(made):
    last, side = place_last(), place_side()
    for at, name in enumerate(("mixed", "grad")):
        ref = made.buffers[name]
        ends = nn(last, ref[SLOT * (len(LATE) - 2) :]).astype(BF16)
        made["row"][ROW_OUT * at : ROW_OUT * (at + 1)] = ends[:ROW_OUT]
        made["cor"][COR_OUT * at : COR_OUT * (at + 1)] = ends[ROW_OUT:]
        beyond = [ref[SLOT * k : SLOT * (k + 1)] for k in (0, 1, 3)]
        picked = nn(side, jnp.concatenate(beyond, axis=0)).astype(BF16)
        made["col"][COL_OUT * at : COL_OUT * (at + 1)] = picked
    made.send("col", "row", "cor")


def early_body(given, made, *scratch):
    places, rest = scratch[:4], scratch[4:]
    made["grads"][...] = attend(given, made, EARLY, early_blocks, None, places, *rest)
    made.send("grads")


def late_body(given, made, pole_ref, *scratch):
    places = [made.buffers[x] for x in ("xw", "cw", "blended", "back")]
    grads = attend(given, made, LATE, late_blocks, pole_ref[0], places, *scratch)
    grads = grads + given["grads"][...]
    tiles = made["tiles"]
    for owner in range(16):
        at = 256 * owner
        if at < WIDTH:
            both = (grads[:, at : at + 128], grads[:, at + 128 : at + 256])
            tiles[owner] = jnp.concatenate(both, axis=0).astype(BF16)
        else:
            tiles[owner] = jnp.zeros((16, 128), BF16)
    made.send("tiles")


def finish_body(given, made):
    finish(
        given,
        made,
        len(LATE),
        *(lambda x=x: given[x] for x in ("xw", "cw", "blended", "back")),
    )
    send_back(made)


def place_body(given, made):
    rows = WIN_LAT * LON_CELLS
    places = [place_out(a) for a in range(BANDS)]
    for at, name in enumerate(("mixed", "grad")):
        parts = {EARLY: given[name + "1"], LATE: given[name + "2"]}

        def window(where):
            part = EARLY if where in EARLY else LATE
            k = part.index(where)
            return parts[part][SLOT * k : SLOT * (k + 1)]

        def band(a):
            return [window((a, b)) for b in range(ACROSS)]

        for a in range(BANDS):
            if a:
                before = band(a - 1)
            else:
                before = [
                    given["row"][ROW_OUT * at : ROW_OUT * (at + 1)],
                    given["cor"][COR_OUT * at : COR_OUT * (at + 1)],
                    window((0, 0))[: SPAN - ROW_OUT - COR_OUT],
                ]
            side = given["col"][COL_OUT * at : COL_OUT * (at + 1)]
            source = jnp.concatenate((*before, *band(a), side), axis=0)
            out = made["all_" + name]
            out[rows * a : rows * (a + 1)] = nn(places[a], source).astype(BF16)
        made.send("all_" + name)


def grads_body(scale, given, made):
    tile = 0
    for name in GRADS:
        ref = made[name]
        for at in range(ref.shape[1] // 128):
            owner, row = tile // 2, RANK * (tile % 2)
            wide = given["tiles"][owner].astype(F32) * scale
            ref[:, 128 * at : 128 * (at + 1)] = wide[row : row + RANK]
            tile += 1
    made.send(*GRADS)


def exchange(tiles, axis):
    return lax.all_to_all(tiles, axis, 0, 0, tiled=True)


def sum_tiles(tiles):
    return jnp.sum(tiles.astype(F32), axis=0).astype(BF16)


def gather_tiles(tile, axis):
    spread = jnp.broadcast_to(tile[None], (lax.axis_size(axis),) + tile.shape)
    return exchange(spread, axis)


def start_total(tiles):
    return exchange(tiles, "lat")


def total_over_mesh(own):
    own = sum_tiles(gather_tiles(sum_tiles(own), "lon"))
    return gather_tiles(own, "lat")


def moved(block, lat_step, lon_step):
    lats, lons = lax.axis_size("lat"), lax.axis_size("lon")
    if lat_step == 0:
        return lax.ppermute(block, "lon", [(i, (i + lon_step) % lons) for i in range(lons)])
    if lon_step == 0:
        return lax.ppermute(block, "lat", [(i, (i + lat_step) % lats) for i in range(lats)])
    route = [
        (i * lons + j, (i + lat_step) % lats * lons + (j + lon_step) % lons)
        for i in range(lats)
        for j in range(lons)
    ]
    return lax.ppermute(block, ("lat", "lon"), route)


def shapes_of(count, *widths):
    return [((SLOT * count, width), BF16) for width in widths]


def scratch_of(count, *widths):
    buffers = [pltpu.VMEM(*x) for x in shapes_of(count, *widths, D, 3 * D, D)]
    return [*buffers, pltpu.VMEM((GROUP, 16, 256), BF16), pltpu.VMEM((CELLS, STACK), F32)]


def shards(
    fine_tokens, cotangent, norm_gain, qkv_weight, qkv_down, qkv_up, out_weight, out_down, out_up
):
    lats, lons = lax.axis_size("lat"), lax.axis_size("lon")
    tokens = fine_tokens.reshape(OWN, D)
    cots = cotangent.reshape(OWN, D)
    pack = jnp.concatenate((qkv_down.T, qkv_up, out_down.T, out_up), axis=1)
    pack = jnp.pad(pack, ((0, PACK - RANK), (0, 0)))
    weights = {
        "gain": norm_gain.reshape(1, D),
        "pack": pack,
        "qkv": qkv_weight,
        "out": out_weight,
    }
    pole = (lax.axis_index("lat") == lats - 1).astype(jnp.int32).reshape(1)
    row, col, cor = call(
        send_body,
        {"x": tokens, "c": cots},
        {
            "row": ((2 * ROW_IN, D), BF16),
            "col": ((2 * COL_IN, D), BF16),
            "cor": ((2 * COR_IN, D), BF16),
        },
        "send",
        near=("row", "col", "cor"),
        flops=10**8,
    )
    col = moved(col, 0, -1)
    row = moved(row, -1, 0)
    cor = moved(cor, -1, -1)
    outs = dict(zip(("mixed", "grad"), shapes_of(len(EARLY), D, D)))
    outs["grads"] = ((RANK, WIDTH), F32)
    scratch = scratch_of(len(EARLY), D, D, D, 3 * D)
    mixed1, grad1, grads = call(
        early_body,
        {"x": tokens, "c": cots, **weights},
        outs,
        "early",
        scratch=scratch,
        flops=4 * 10**9,
    )
    outs = dict(zip(("xw", "cw", "blended", "back"), shapes_of(len(LATE), D, D, D, 3 * D)))
    outs["tiles"] = ((16, 16, 128), BF16)
    scratch = scratch_of(len(LATE))
    xw, cw, blended, back, tiles = call(
        late_body,
        {
            "pole": pole,
            "x": tokens,
            "c": cots,
            **weights,
            "grads": grads,
            "row_in": row,
            "col_in": col,
            "cor_in": cor,
        },
        outs,
        "late",
        scratch=scratch,
        scalars=1,
        near=("row_in", "col_in", "cor_in"),
        flops=8 * 10**9,
    )
    own = start_total(tiles)
    outs = dict(zip(("mixed", "grad"), shapes_of(len(LATE), D, D)))
    outs["row"] = ((2 * ROW_OUT, D), BF16)
    outs["col"] = ((2 * COL_OUT, D), BF16)
    outs["cor"] = ((2 * COR_OUT, D), BF16)
    mixed2, grad2, row, col, cor = call(
        finish_body,
        {
            "xw": xw,
            "blended": blended,
            "pack": pack,
            "out": out_weight,
            "back": back,
            "qkv": qkv_weight,
            "gain": weights["gain"],
            "cw": cw,
        },
        outs,
        "finish",
        near=("row", "col", "cor"),
        flops=2 * 10**9,
    )
    col = moved(col, 0, 1)
    own, row, cor = lax.optimization_barrier((own, row, cor))
    row = moved(row, 1, 0)
    cor = moved(cor, 1, 1)
    tiles = total_over_mesh(own)
    mixed, grad = call(
        place_body,
        {
            "mixed1": mixed1,
            "mixed2": mixed2,
            "row": row,
            "cor": cor,
            "col": col,
            "grad1": grad1,
            "grad2": grad2,
        },
        {"all_mixed": ((OWN, D), BF16), "all_grad": ((OWN, D), BF16)},
        "place",
        near=("row", "col", "cor"),
        flops=10**9,
    )
    scale = 1.0 / math.sqrt(OWN * lats * lons)

    def last_grads(*refs):
        grads_body(scale, *refs)

    grads = call(
        last_grads,
        {"tiles": tiles},
        dict(zip(GRADS, (((RANK, width), F32) for width in (D, 3 * D, D, D)))),
        "grads",
    )
    shape = (LAT_CELLS, LON_CELLS, D)
    return (
        mixed.reshape(shape),
        grad.reshape(shape),
        grads[0].T,
        grads[1],
        grads[2].T,
        grads[3],
    )


def solution(mesh):
    in_specs = (P("lat", "lon", None), P("lat", "lon", None), P(), P(), P(), P(), P(), P(), P())
    out_specs = (P("lat", "lon", None), P("lat", "lon", None), P(), P(), P(), P())
    return jax.shard_map(shards, mesh=mesh, in_specs=in_specs, out_specs=out_specs, check_vma=False)
```

```python
import math

import jax
import jax.numpy as jnp
from jax import lax
from jax.experimental import pallas as pl
from jax.experimental.pallas import tpu as pltpu
from jax.sharding import PartitionSpec as P

HEADS = 16
WIN_LAT = 6
WIN_LON = 12
HALF_LAT = WIN_LAT // 2
HALF_LON = WIN_LON // 2
LAT_CELLS = 18
LON_CELLS = 24
D = 512
RANK = 8
CELLS = WIN_LAT * WIN_LON
SLOT = 80
BANDS = LAT_CELLS // WIN_LAT
ACROSS = LON_CELLS // WIN_LON
WINDOWS = BANDS * ACROSS
EARLY = ((0, 0), (1, 0))
LATE = ((0, 1), (1, 1), (2, 0), (2, 1))
ORDER = EARLY + LATE
SPAN = 160
TOKENS = WINDOWS * SLOT
OWN = LAT_CELLS * LON_CELLS
HEAD_WIDTH = D // HEADS
GROUP = 256 // HEAD_WIDTH
GROUPS = HEADS // GROUP
STACK = GROUP * SLOT
ROW_IN, COL_IN, COR_IN = 80, 112, 32
COL_FROM, COL_PART = (16, 48, 64), 48
PACK = 2 * RANK
WIDTH = 6 * D
ROW_OUT, COL_OUT, COR_OUT = 64, 96, 32
BF16 = jnp.bfloat16
F32 = jnp.float32
VMEM_ASKED = {"send": 60, "early": 60, "late": 52, "place": 52, "grads": 52}
GRADS = ("qkv_down", "qkv_up", "out_down", "out_up")
FIXED = ("x", "c", "gain", "qkv", "out")


def own_from(a):
    return 64 + 144 * a


def marks_at(shape, source):
    row = lax.broadcasted_iota(jnp.int32, shape, 0)
    lane = lax.broadcasted_iota(jnp.int32, shape, 1)
    return jnp.where(lane == source(row), 1.0, 0.0).astype(BF16)


def over(value, divisor):
    factor, shift = {6: (10923, 16), 12: (10923, 17), 18: (7282, 17), 24: (10923, 18)}[divisor]
    return jnp.right_shift(value * factor, shift)


def pick(test, one, other):
    return jnp.where(test, one, other)


def place_send():
    def source(row):
        at = pick(row < COL_IN, row, row - COL_IN)
        r = over(at, HALF_LON)
        ends = pick(row < COL_IN, HALF_LON * LAT_CELLS, HALF_LON * HALF_LAT)
        return pick(at < ends, LON_CELLS * r + at - HALF_LON * r, -1)

    return marks_at((COL_IN + COR_IN, OWN), source)


def place_in(window, width):
    a, b = window

    def source(cell):
        r = over(cell, WIN_LON)
        c = cell - WIN_LON * r
        row, col = WIN_LAT * a + r + HALF_LAT, WIN_LON * b + c + HALF_LON
        at = LON_CELLS * row + col - own_from(a)
        if b == ACROSS - 1:
            side = SPAN + HALF_LON * row + col - LON_CELLS - COL_FROM[a]
            corner = SPAN + COL_PART + HALF_LON * (row - LAT_CELLS) + col - LON_CELLS
            at = pick(col < LON_CELLS, at, pick(row < LAT_CELLS, side, corner))
        return pick(cell < CELLS, at, -1)

    return marks_at((SLOT, width), source)


def place_last():
    def source(row):
        rho = over(row, LON_CELLS - HALF_LON)
        j = row - (LON_CELLS - HALF_LON) * rho
        cell = WIN_LON * (HALF_LAT + rho) + j
        along = pick(j < WIN_LON, cell, cell + SLOT - WIN_LON)
        along = pick(row < (LON_CELLS - HALF_LON) * HALF_LAT, along, -1)
        at = row - ROW_OUT
        rho = over(jnp.maximum(at, 0), HALF_LON)
        corner = SLOT + WIN_LON * (HALF_LAT + rho) + HALF_LON + at - HALF_LON * rho
        corner = pick(at < HALF_LON * HALF_LAT, corner, -1)
        return pick(row < ROW_OUT, along, corner)

    return marks_at((ROW_OUT + COR_OUT, ACROSS * SLOT), source)


def place_side():
    def source(row):
        i = over(row, HALF_LON)
        a = over(i, WIN_LAT)
        cell = WIN_LON * (i - WIN_LAT * a) + HALF_LON + row - HALF_LON * i
        return pick(row < HALF_LON * (LAT_CELLS - HALF_LAT), SLOT * a + cell, -1)

    return marks_at((COL_OUT, BANDS * SLOT), source)


def place_out(at):
    def source(row):
        r = over(row, LON_CELLS)
        col = row - LON_CELLS * r
        i, j = WIN_LAT * at + r - HALF_LAT, col - HALF_LON
        late = r >= HALF_LAT
        cell = WIN_LON * pick(late, r - HALF_LAT, r + HALF_LAT) + j
        cell = pick(j < WIN_LON, cell, cell + SLOT - WIN_LON)
        inner = pick(late, SPAN + cell, cell)
        edge = 2 * SPAN + HALF_LON * i + col
        if at == 0:
            inner = pick(late, inner, (LON_CELLS - HALF_LON) * r + j)
            edge = pick(late, edge, ROW_OUT + HALF_LON * r + col)
        return pick(j < 0, edge, inner)

    return marks_at((WIN_LAT * LON_CELLS, 2 * SPAN + COL_OUT), source)


def head_marks():
    lane = lax.broadcasted_iota(jnp.int32, (16, 256), 1)
    heads = [
        jnp.where(jnp.right_shift(lane, 5) == head, 1.0, 0.0).astype(BF16)
        for head in range(GROUP)
    ]
    return jnp.stack(heads, axis=0)


def nn(left, right):
    return lax.dot_general(left, right, (((1,), (0,)), ((), ())), preferred_element_type=F32)


def nt(left, right):
    return lax.dot_general(left, right, (((1,), (1,)), ((), ())), preferred_element_type=F32)


class Staged:
    def __init__(self, names, outside, buffers, sem):
        self.copies = {x: (outside[x], buffers[x], sem[x]) for x in names if x in buffers}
        self.buffers = {x: buffers.get(x, outside[x]) for x in names}
        self.open = {}

    def fetch(self):
        for name, (ref, buffer, sem) in self.copies.items():
            self.open[name] = pltpu.make_async_copy(ref, buffer, sem)
            self.open[name].start()

    def __getitem__(self, name):
        if name in self.open:
            self.open.pop(name).wait()
        return self.buffers[name]

    def send(self, *names):
        for name in names:
            if name not in self.copies:
                continue
            ref, buffer, sem = self.copies[name]
            self.open[name] = pltpu.make_async_copy(buffer, ref, sem)
            self.open[name].start()

    def close(self):
        for name in list(self.open):
            self.open.pop(name).wait()


def call(body, ins, outs, name, scratch=(), scalars=0, near=(), keep=(), flops=0):
    arrays = list(ins.values())
    outs = dict(outs, **{x + "_kept": (ins[x].shape, ins[x].dtype) for x in keep})
    in_names, out_names = list(ins)[scalars:], list(outs)
    near = (*near, *(x + "_kept" for x in keep))
    shapes = [jax.ShapeDtypeStruct(shape, dtype) for shape, dtype in outs.values()]
    names = in_names + out_names
    far = [x for x in names if x not in near]
    own = [x for x in far if x not in keep]
    kinds = dict(zip(names, arrays[scalars:] + shapes))

    def kernel(*refs):
        heads, refs = refs[:scalars], refs[scalars:]
        outside, refs = dict(zip(names, refs)), refs[len(names) :]
        buffers, refs = dict(zip(own, refs)), refs[len(own) :]
        buffers.update({x: outside[x + "_kept"] for x in keep})
        sems, rest = refs[0], refs[1:]
        sem = {x: sems.at[at] for at, x in enumerate(far)}
        given = Staged(in_names, outside, buffers, sem)
        made = Staged(out_names, outside, buffers, sem)
        given.fetch()
        body(given, made, *heads, *rest)
        given.close()
        made.close()

    def spec(x):
        if x in near:
            return pl.BlockSpec(memory_space=pltpu.VMEM)
        return pl.BlockSpec(memory_space=pltpu.HBM if x in FIXED else pl.ANY)

    return pl.pallas_call(
        kernel,
        out_shape=shapes,
        in_specs=[pl.BlockSpec(memory_space=pltpu.SMEM)] * scalars + [spec(x) for x in in_names],
        out_specs=[spec(x) for x in out_names],
        scratch_shapes=[pltpu.VMEM(kinds[x].shape, kinds[x].dtype) for x in own]
        + [pltpu.SemaphoreType.DMA((max(len(far), 1),))]
        + list(scratch),
        compiler_params=pltpu.CompilerParams(vmem_limit_bytes=VMEM_ASKED[name] << 20),
        cost_estimate=pl.CostEstimate(
            flops=flops, bytes_accessed=4 * 1024 * 1024, transcendentals=0
        ),
        name=name,
    )(*arrays)


def send_body(given, made):
    for at, name in enumerate(("x", "c")):
        made["row"][ROW_IN * at : ROW_IN * (at + 1)] = given[name][:ROW_IN]
    made.send("row")
    place = place_send()
    for at, name in enumerate(("x", "c")):
        picked = nn(place, given[name][...]).astype(BF16)
        made["col"][COL_IN * at : COL_IN * (at + 1)] = picked[:COL_IN]
        made["cor"][COR_IN * at : COR_IN * (at + 1)] = picked[COL_IN:]
    made.send("col", "cor")


def split_heads(block, marks):
    tiles = block.reshape(1, SLOT // 16, 16, 256) * marks[:, None]
    return tiles.reshape(STACK, 256)


def join_heads(stacked):
    lane = lax.broadcasted_iota(jnp.int32, (SLOT, 128), 1)
    parts = [stacked[SLOT * h : SLOT * (h + 1)] for h in range(4)]
    low = jnp.where(lane < 32, parts[0], parts[1])
    high = jnp.where(lane < 96, parts[2], parts[3])
    return jnp.where(lane < 64, low, high)


def per_query(weights, block):
    turned = weights.T
    half = STACK // 2
    return jnp.concatenate(
        (
            join_heads(nn(turned[:half], block[:, :128])),
            join_heads(nn(turned[half:], block[:, 128:])),
        ),
        axis=1,
    )


def adapters(pack_ref):
    return (
        pack_ref[:, :D],
        pack_ref[:, D : 4 * D],
        pack_ref[:, 4 * D : 5 * D],
        pack_ref[:, 5 * D :],
    )


def attend(given, made, windows, blocks, ended, pole, tokens, cots, hidden, packed, bblend, blended_ref, back_ref, marks_ref, apart_ref):
    count = len(windows)
    for first in range(0, count, 2):
        rows = pl.ds(SLOT * first, 2 * SLOT)
        blocks(given, tokens, cots, first)
        wide = tokens[rows].astype(F32)
        center = wide - jnp.mean(wide, axis=-1, keepdims=True)
        spread = jnp.mean(center * center, axis=-1, keepdims=True)
        normed = (center * lax.rsqrt(spread + 1e-05) * given["gain"][...]).astype(BF16)
        hidden[rows] = normed
        down, up, odown, oup = adapters(given["pack"])
        low = nt(normed, down).astype(BF16)
        packed[rows] = (nn(normed, given["qkv"][...]) + nn(low, up)).astype(BF16)
        cot = cots[rows]
        back_low = nt(cot, oup).astype(BF16)
        bblend[rows] = (nt(cot, given["out"][...]) + nn(back_low, odown)).astype(BF16)

    marks_ref[...] = head_marks()
    rest = jnp.zeros((SLOT - CELLS, STACK), F32)
    scale = 1.0 / math.sqrt(HEAD_WIDTH)
    marks = marks_ref[...]
    if pole is not None:
        key_late = lax.broadcasted_iota(jnp.int32, (CELLS, STACK), 0) >= CELLS // 2
        query_at = lax.rem(lax.broadcasted_iota(jnp.int32, (CELLS, STACK), 1), SLOT)
        cut = jnp.where(pole > 0, -1e30, 0.0)
        apart_ref[...] = (key_late != (query_at >= CELLS // 2)).astype(F32) * cut

    for w, (a, _) in enumerate(windows):
        rows = pl.ds(w * SLOT, SLOT)
        for g in range(GROUPS):
            at = 256 * g
            query = packed[rows, at : at + 256]
            key = packed[rows, D + at : D + at + 256]
            value = packed[rows, 2 * D + at : 2 * D + at + 256]
            back = bblend[rows, at : at + 256]
            queries = split_heads(query, marks)
            backs = split_heads(back, marks)
            scores = nt(key, queries)[:CELLS]
            if a == BANDS - 1:
                scores = scores + apart_ref[...]
            top = jnp.max(scores, axis=0, keepdims=True)
            exponent = jnp.exp2((scores - top) * (scale * math.log2(math.e)))
            weights = exponent * (1.0 / jnp.sum(exponent, axis=0, keepdims=True))
            rounded = jnp.concatenate((weights, rest), axis=0).astype(BF16)
            blended_ref[rows, at : at + 256] = per_query(rounded, value).astype(BF16)
            back_weights = nt(value, backs)[:CELLS].astype(BF16).astype(F32)
            total = jnp.sum(weights * back_weights, axis=0, keepdims=True)
            back_scores = (weights * scale) * (back_weights - total)
            back_scores = jnp.concatenate((back_scores, rest), axis=0).astype(BF16)
            back_ref[rows, at : at + 256] = per_query(back_scores, key).astype(BF16)
            back_ref[rows, D + at : D + at + 256] = nn(back_scores, queries).astype(BF16)
            back_ref[rows, 2 * D + at : 2 * D + at + 256] = nn(rounded, backs).astype(BF16)

    for first in range(0, count, 2):
        rows = pl.ds(SLOT * first, 2 * SLOT)
        wide = tokens[rows].astype(F32)
        blended = blended_ref[rows]
        low = nt(blended, odown).astype(BF16)
        update = (nn(blended, given["out"][...]) + nn(low, oup)).astype(BF16)
        made["mixed"][rows] = (wide + update.astype(F32)).astype(BF16)
        back = back_ref[rows]
        back_low = nt(back, up).astype(BF16)
        back_hidden = nt(back, given["qkv"][...]) + nn(back_low, down)
        center = wide - jnp.mean(wide, axis=-1, keepdims=True)
        spread = jnp.mean(center * center, axis=-1, keepdims=True)
        inverse = lax.rsqrt(spread + 1e-05)
        normed = center * inverse
        scaled = back_hidden * given["gain"][...]
        along = jnp.mean(scaled * normed, axis=-1, keepdims=True)
        across = jnp.mean(scaled, axis=-1, keepdims=True)
        change = (inverse * (scaled - across - normed * along)).astype(BF16).astype(F32)
        made["grad"][rows] = (cots[rows].astype(F32) + change).astype(BF16)
    made.send("mixed", "grad")
    ended(made)
    cot = cots[...]
    blended = blended_ref[...]
    back = back_ref[...]
    return jnp.concatenate(
        (
            nn(nt(up, back).astype(BF16), hidden[...])[:RANK],
            nn(nt(down, hidden[...]).astype(BF16), back)[:RANK],
            nn(nt(oup, cot).astype(BF16), blended)[:RANK],
            nn(nt(odown, blended).astype(BF16), cot)[:RANK],
        ),
        axis=1,
    )


def early_blocks(given, tokens, cots, first):
    for k in range(first, first + 2):
        begin = own_from(EARLY[k][0])
        place = place_in(EARLY[k], SPAN)
        for source, into in (("x", tokens), ("c", cots)):
            own = given[source][begin : begin + SPAN]
            into[SLOT * k : SLOT * (k + 1)] = nn(place, own).astype(BF16)


def late_blocks(given, tokens, cots, first):
    for k in range(first, first + 2):
        a, b = LATE[k]
        begin = own_from(a)
        place = place_in(LATE[k], SPAN + COL_PART + COR_IN)
        for at, (source, into) in enumerate((("x", tokens), ("c", cots))):
            if a < BANDS - 1:
                own = given[source][begin : begin + SPAN]
            else:
                row = given["row_in"][ROW_IN * at : ROW_IN * (at + 1)]
                own = jnp.concatenate((given[source][begin:], row), axis=0)
            side = given["col_in"][pl.ds(COL_IN * at + COL_FROM[a], COL_PART)]
            corner = given["cor_in"][COR_IN * at : COR_IN * (at + 1)]
            block = jnp.concatenate((own, side, corner), axis=0)
            into[SLOT * k : SLOT * (k + 1)] = nn(place, block).astype(BF16)


def early_ended(made):
    pass


def late_ended(made):
    last, side = place_last(), place_side()
    for at, name in enumerate(("mixed", "grad")):
        ref = made.buffers[name]
        ends = nn(last, ref[SLOT * (len(LATE) - 2) :]).astype(BF16)
        made["row"][ROW_OUT * at : ROW_OUT * (at + 1)] = ends[:ROW_OUT]
        made["cor"][COR_OUT * at : COR_OUT * (at + 1)] = ends[ROW_OUT:]
        beyond = [ref[SLOT * k : SLOT * (k + 1)] for k in (0, 1, 3)]
        picked = nn(side, jnp.concatenate(beyond, axis=0)).astype(BF16)
        made["col"][COL_OUT * at : COL_OUT * (at + 1)] = picked
    made.send("col", "row", "cor")


def early_body(given, made, *scratch):
    grads = attend(given, made, EARLY, early_blocks, early_ended, None, *scratch)
    made["grads"][...] = grads
    made.send("grads")


def late_body(given, made, pole_ref, *scratch):
    grads = attend(given, made, LATE, late_blocks, late_ended, pole_ref[0], *scratch)
    grads = grads + given["grads"][...]
    tiles = made["tiles"]
    for owner in range(16):
        at = 256 * owner
        if at < WIDTH:
            both = (grads[:, at : at + 128], grads[:, at + 128 : at + 256])
            tiles[owner] = jnp.concatenate(both, axis=0).astype(BF16)
        else:
            tiles[owner] = jnp.zeros((16, 128), BF16)
    made.send("tiles")


def place_body(given, made):
    rows = WIN_LAT * LON_CELLS
    places = [place_out(a) for a in range(BANDS)]
    for at, name in enumerate(("mixed", "grad")):
        parts = {EARLY: given[name + "1"], LATE: given[name + "2"]}

        def window(where):
            part = EARLY if where in EARLY else LATE
            k = part.index(where)
            return parts[part][SLOT * k : SLOT * (k + 1)]

        def band(a):
            return [window((a, b)) for b in range(ACROSS)]

        for a in range(BANDS):
            if a:
                before = band(a - 1)
            else:
                before = [
                    given["row"][ROW_OUT * at : ROW_OUT * (at + 1)],
                    given["cor"][COR_OUT * at : COR_OUT * (at + 1)],
                    window((0, 0))[: SPAN - ROW_OUT - COR_OUT],
                ]
            side = given["col"][COL_OUT * at : COL_OUT * (at + 1)]
            source = jnp.concatenate((*before, *band(a), side), axis=0)
            out = made["all_" + name]
            out[rows * a : rows * (a + 1)] = nn(places[a], source).astype(BF16)
        made.send("all_" + name)


def grads_body(scale, given, made):
    tile = 0
    for name in GRADS:
        ref = made[name]
        for at in range(ref.shape[1] // 128):
            owner, row = tile // 2, RANK * (tile % 2)
            wide = given["tiles"][owner].astype(F32) * scale
            ref[:, 128 * at : 128 * (at + 1)] = wide[row : row + RANK]
            tile += 1
    made.send(*GRADS)


def exchange(tiles, axis):
    return lax.all_to_all(tiles, axis, 0, 0, tiled=True)


def sum_tiles(tiles):
    return jnp.sum(tiles.astype(F32), axis=0).astype(BF16)


def gather_tiles(tile, axis):
    spread = jnp.broadcast_to(tile[None], (lax.axis_size(axis),) + tile.shape)
    return exchange(spread, axis)


def start_total(tiles):
    return exchange(tiles, "lat")


def total_over_mesh(own):
    own = sum_tiles(gather_tiles(sum_tiles(own), "lon"))
    return gather_tiles(own, "lat")


def moved(block, lat_step, lon_step):
    lats, lons = lax.axis_size("lat"), lax.axis_size("lon")
    if lat_step == 0:
        return lax.ppermute(block, "lon", [(i, (i + lon_step) % lons) for i in range(lons)])
    if lon_step == 0:
        return lax.ppermute(block, "lat", [(i, (i + lat_step) % lats) for i in range(lats)])
    route = [
        (i * lons + j, (i + lat_step) % lats * lons + (j + lon_step) % lons)
        for i in range(lats)
        for j in range(lons)
    ]
    return lax.ppermute(block, ("lat", "lon"), route)


def attended(count, last):
    outs = {"mixed": ((SLOT * count, D), BF16), "grad": ((SLOT * count, D), BF16)}
    outs.update(last)
    widths = (D, D, D, 3 * D, D, D, 3 * D)
    scratch = [pltpu.VMEM((SLOT * count, width), BF16) for width in widths]
    return outs, scratch + [pltpu.VMEM((GROUP, 16, 256), BF16), pltpu.VMEM((CELLS, STACK), F32)]


def shards(
    fine_tokens, cotangent, norm_gain, qkv_weight, qkv_down, qkv_up, out_weight, out_down, out_up
):
    lats, lons = lax.axis_size("lat"), lax.axis_size("lon")
    tokens = fine_tokens.reshape(OWN, D)
    cots = cotangent.reshape(OWN, D)
    pack = jnp.concatenate((qkv_down.T, qkv_up, out_down.T, out_up), axis=1)
    pack = jnp.pad(pack, ((0, PACK - RANK), (0, 0)))
    weights = {
        "gain": norm_gain.reshape(1, D),
        "pack": pack,
        "qkv": qkv_weight,
        "out": out_weight,
    }
    pole = (lax.axis_index("lat") == lats - 1).astype(jnp.int32).reshape(1)
    row, col, cor = call(
        send_body,
        {"x": tokens, "c": cots},
        {
            "row": ((2 * ROW_IN, D), BF16),
            "col": ((2 * COL_IN, D), BF16),
            "cor": ((2 * COR_IN, D), BF16),
        },
        "send",
        flops=10**8,
    )
    col = moved(col, 0, -1)
    row = moved(row, -1, 0)
    cor = moved(cor, -1, -1)
    outs, scratch = attended(len(EARLY), {"grads": ((RANK, WIDTH), F32)})
    mixed1, grad1, grads = call(
        early_body,
        {"x": tokens, "c": cots, **weights},
        outs,
        "early",
        scratch=scratch,
        flops=4 * 10**9,
    )
    last = {
        "tiles": ((16, 16, 128), BF16),
        "row": ((2 * ROW_OUT, D), BF16),
        "col": ((2 * COL_OUT, D), BF16),
        "cor": ((2 * COR_OUT, D), BF16),
    }
    outs, scratch = attended(len(LATE), last)
    mixed2, grad2, tiles, row, col, cor = call(
        late_body,
        {
            "pole": pole,
            "x": tokens,
            "c": cots,
            **weights,
            "grads": grads,
            "row_in": row,
            "col_in": col,
            "cor_in": cor,
        },
        outs,
        "late",
        scratch=scratch,
        scalars=1,
        near=("row_in", "col_in", "cor_in"),
        flops=8 * 10**9,
    )
    own = start_total(tiles)
    col = moved(col, 0, 1)
    own, row, cor = lax.optimization_barrier((own, row, cor))
    row = moved(row, 1, 0)
    cor = moved(cor, 1, 1)
    tiles = total_over_mesh(own)
    mixed, grad = call(
        place_body,
        {
            "mixed1": mixed1,
            "mixed2": mixed2,
            "row": row,
            "cor": cor,
            "col": col,
            "grad1": grad1,
            "grad2": grad2,
        },
        {"all_mixed": ((OWN, D), BF16), "all_grad": ((OWN, D), BF16)},
        "place",
        near=("row", "col", "cor"),
        flops=10**9,
    )
    scale = 1.0 / math.sqrt(OWN * lats * lons)

    def last_grads(*refs):
        grads_body(scale, *refs)

    grads = call(
        last_grads,
        {"tiles": tiles},
        dict(zip(GRADS, (((RANK, width), F32) for width in (D, 3 * D, D, D)))),
        "grads",
    )
    shape = (LAT_CELLS, LON_CELLS, D)
    return (
        mixed.reshape(shape),
        grad.reshape(shape),
        grads[0].T,
        grads[1],
        grads[2].T,
        grads[3],
    )


def solution(mesh):
    in_specs = (P("lat", "lon", None), P("lat", "lon", None), P(), P(), P(), P(), P(), P(), P())
    out_specs = (P("lat", "lon", None), P("lat", "lon", None), P(), P(), P(), P())
    return jax.shard_map(shards, mesh=mesh, in_specs=in_specs, out_specs=out_specs, check_vma=False)
```
